512 devices in a mesh: shard: 32 (over y, x), expert: 8 (over z), replica: 2 (over core).
Axes of the slice: x: 4, y: 8, z: 8, core: 2. Of those that a mesh axis runs over, the one named last changes fastest.
Arguments:
- momentum: float32 [32, 3584, 384], P('expert', 'shard'), may hold values from -120 to 120
- gradient: bfloat16 [32, 3584, 384], P('expert', 'shard'), may hold values from -6 to 6
- weight: bfloat16 [32, 3584, 384], P('expert', 'shard'), may hold values from -6 to 6
Outputs:
- new_momentum: float32 [32, 3584, 384], P('expert', 'shard')
- update: bfloat16 [32, 3584, 384], P('expert', 'shard')
The draws below stay inside these ranges and needn't reach their ends.
All inputs are finite; a program needn't handle non-finite values.
Results may differ from the reference program's by a relative error of at most 0.015.
The reference program's roundings to bfloat16 on the way (of `rounded`, `initial`, `iterate`, `gram` and `polynomial`) count: a program that leaves them out, or rounds other values in their place, can miss the bound.
Values may be sent and summed in bfloat16 or wider, within the bound.
No kernel may reach another device: no remote copies, remote signals or barrier semaphores. Data moves between devices by JAX's collectives and lax.ppermute only.
A program may use at most 64 MiB of HBM per device.

```python
import math
import jax
import jax.numpy as jnp
from jax import lax

D = 3584
C = 384
ITERS = 5
NMAT = 32


def draw_momentum(key, part):
    key = jax.random.fold_in(key, 7)
    key_rows, key_cols, key_main = jax.random.split(key, 3)
    row_scale = jnp.exp(jax.random.uniform(key_rows, (NMAT, D, 1), jnp.float32, 0.0, math.log(10.0)))
    col_scale = jnp.exp(jax.random.uniform(key_cols, (NMAT, 1, C), jnp.float32, 0.0, math.log(10.0)))
    rising = (1.0 + 2.0 * jnp.arange(D, dtype=jnp.float32) / (D - 1.0)).reshape(1, D, 1)
    entries = jnp.clip(jax.random.normal(key_main, (NMAT, D, C), jnp.float32), -4.0, 4.0)
    return (0.1 * entries * row_scale * rising * col_scale).astype(jnp.float32)


def levels(key, extent, cuts, smallest, top_value):
    factor_of, own = 1.0, jax.random.fold_in(key, 6)
    for position, parts in cuts:
        draws = jnp.exp(jax.random.uniform(jax.random.fold_in(own, position), (parts,), jnp.float32, smallest / len(cuts), top_value / len(cuts)))
        factor_of = factor_of * jnp.repeat(draws, extent[position] // parts).reshape([-1 if axis == position else 1 for axis in range(len(extent))])
    return factor_of


def bell_draw(key, dims, scale, bound, cuts=(), kind=jnp.bfloat16):
    values = jax.random.normal(key, dims, jnp.float32) * scale
    if len(cuts) > 0:
        values = levels(key, dims, cuts, -0.22, 0.18) * values
    return jnp.clip(values, min=-bound, max=bound).astype(kind)


def setup_inputs(seed: int = 0) -> dict:
    key_of = jax.random.split(jax.random.key(seed), 4)
    momentum = draw_momentum(jax.random.fold_in(key_of[3], 71), 0)
    gradient = bell_draw(key_of[1], (NMAT, D, C), 1.0, 6.0, ((0, 8), (1, 32)))
    weight = bell_draw(key_of[2], (NMAT, D, C), 1.0, 6.0, ((0, 8), (1, 32)))
    return dict(momentum=momentum, gradient=gradient, weight=weight)


MOMENTUM_COEF = 0.95
NORM_EPS = 1e-07
A_COEF = 3.4445
B_COEF = -4.775
C_COEF = 2.0315
WEIGHT_DECAY = 0.1

def orthogonalize(iterate):
    for iteration in range(ITERS):
        iterate = lax.optimization_barrier(iterate)
        gram = jnp.dot(iterate.T, iterate, preferred_element_type=jnp.float32).astype(jnp.bfloat16)
        gram = lax.optimization_barrier(gram)
        square = jnp.dot(gram, gram, preferred_element_type=jnp.float32)
        polynomial = (B_COEF * gram.astype(jnp.float32) + C_COEF * square).astype(jnp.bfloat16)
        product = jnp.dot(iterate, polynomial, preferred_element_type=jnp.float32)
        iterate = (A_COEF * iterate.astype(jnp.float32) + product).astype(jnp.bfloat16)
    return lax.optimization_barrier(iterate)

def one_matrix(operands):
    momentum, gradient, weight = operands
    new_momentum = MOMENTUM_COEF * momentum + gradient.astype(jnp.float32)
    rounded = new_momentum.astype(jnp.bfloat16)
    widened = lax.optimization_barrier(rounded).astype(jnp.float32)
    frobenius = jnp.sqrt(jnp.sum(widened * widened))
    initial = (widened / (frobenius + NORM_EPS)).astype(jnp.bfloat16)
    finished = orthogonalize(initial)
    update_scale = 0.2 * math.sqrt(max(D, C))
    update = (update_scale * finished.astype(jnp.float32) + WEIGHT_DECAY * weight.astype(jnp.float32)).astype(jnp.bfloat16)
    return (new_momentum, update)

def reference(momentum, gradient, weight):
    new_momentum, update = lax.map(one_matrix, (momentum, gradient, weight))
    return (new_momentum, update)
```

```python
import math

import jax
import jax.numpy as jnp
from jax import lax
from jax.experimental import pallas as pl
from jax.experimental.pallas import tpu as pltpu
from jax.sharding import Mesh
from jax.sharding import PartitionSpec as P

D = 3584
C = 384
ITERS = 5
BLK = 128

MOMENTUM_COEF = 0.95
NORM_EPS = 1e-07
A_COEF = 3.4445
B_COEF = -4.775
C_COEF = 2.0315
WEIGHT_DECAY = 0.1

f32 = jnp.float32
bf16 = jnp.bfloat16


def dot(a, b):
    return jnp.dot(a, b, preferred_element_type=f32)


def split(value):
    high = value.astype(bf16)
    low = (value - high.astype(f32)).astype(bf16)
    return high, low


def momentum_kernel(m_ref, g_ref, nm_ref, r_ref):
    new = MOMENTUM_COEF * m_ref[...] + g_ref[...].astype(f32)
    nm_ref[...] = new
    r_ref[...] = new.astype(bf16)


def gram_kernel(core_ref, r_ref, out_ref):
    rows = r_ref[...]

    def cross(i, j0, j1):
        return lax.dot_general(
            rows[:, i * BLK : (i + 1) * BLK],
            rows[:, j0 * BLK : j1 * BLK],
            (((0,), (0,)), ((), ())),
            preferred_element_type=f32,
        )

    @pl.when(core_ref[0] == 0)
    def _():
        top = cross(0, 0, 3)
        for j in range(3):
            out_ref[j] = top[:, j * BLK : (j + 1) * BLK]

    @pl.when(core_ref[0] != 0)
    def _():
        middle = cross(1, 1, 3)
        out_ref[0] = middle[:, :BLK]
        out_ref[1] = middle[:, BLK:]
        out_ref[2] = cross(2, 2, 3)


def chain_kernel(blocks_ref, r_ref, out_ref):
    b = [blocks_ref[i] for i in range(6)]
    gram = jnp.concatenate(
        [
            jnp.concatenate([b[0], b[1], b[2]], axis=1),
            jnp.concatenate([b[1].T, b[3], b[4]], axis=1),
            jnp.concatenate([b[2].T, b[4].T, b[5]], axis=1),
        ],
        axis=0,
    )
    row = lax.broadcasted_iota(jnp.int32, (BLK, BLK), 0)
    col = lax.broadcasted_iota(jnp.int32, (BLK, BLK), 1)
    diagonal = jnp.where(row == col, b[0] + b[3] + b[5], 0.0)
    total = jnp.sum(jnp.sum(diagonal, axis=1, keepdims=True), axis=0, keepdims=True)
    norm = jnp.sqrt(total) + NORM_EPS
    gram = gram / (norm * norm)
    iterate = (r_ref[...].astype(f32) / norm).astype(bf16)
    for iteration in range(ITERS):
        g = gram.astype(bf16)
        poly = (B_COEF * g.astype(f32) + C_COEF * dot(g, g)).astype(bf16)
        iterate = (A_COEF * iterate.astype(f32) + dot(iterate, poly)).astype(bf16)
        if iteration < ITERS - 1:
            high, low = split(gram)
            half = A_COEF * gram + (dot(poly, high) + dot(poly, low))
            high, low = split(half)
            gram = A_COEF * half + (dot(high, poly) + dot(low, poly))
    out_ref[...] = iterate


def update_kernel(x_ref, w_ref, out_ref):
    scale = 0.2 * math.sqrt(max(D, C))
    out_ref[...] = (
        scale * x_ref[...].astype(f32) + WEIGHT_DECAY * w_ref[...].astype(f32)
    ).astype(bf16)


def body(momentum, gradient, weight):
    mats, rows, _ = momentum.shape
    shape = jax.ShapeDtypeStruct
    new_momentum, rounded = pl.pallas_call(
        momentum_kernel,
        out_shape=(shape(momentum.shape, f32), shape(momentum.shape, bf16)),
    )(momentum, gradient)
    owned = lax.all_to_all(rounded, "x", split_axis=0, concat_axis=0, tiled=True)
    owned = owned.reshape(mats * rows, C)
    core = lax.axis_index("replica").astype(jnp.int32).reshape(1)
    partial = pl.pallas_call(
        gram_kernel,
        out_shape=shape((3, BLK, BLK), f32),
        in_specs=[
            pl.BlockSpec(memory_space=pltpu.SMEM),
            pl.BlockSpec(memory_space=pltpu.VMEM),
        ],
    )(core, owned)
    pieces = partial.reshape(8, 3 * BLK // 8, BLK)
    pieces = lax.all_to_all(pieces, "y", split_axis=0, concat_axis=0, tiled=True)
    mine = jnp.sum(pieces, axis=0)
    half = lax.all_gather(mine, "y", axis=0, tiled=True)
    blocks = lax.all_gather(half, "replica", axis=0, tiled=True).reshape(6, BLK, BLK)
    final = pl.pallas_call(
        chain_kernel,
        out_shape=shape((mats * rows, C), bf16),
    )(blocks, owned)
    back = final.reshape(mats, rows, C)
    back = lax.all_to_all(back, "x", split_axis=0, concat_axis=0, tiled=True)
    update = pl.pallas_call(
        update_kernel,
        out_shape=shape(weight.shape, bf16),
    )(back, weight)
    return (new_momentum, update)


def solution(mesh):
    devices = mesh.devices.reshape(8, 4, 8, 2)
    grid = Mesh(devices, ("y", "x", "expert", "replica"))
    placed = P("expert", ("y", "x"), None)
    return jax.shard_map(
        body,
        mesh=grid,
        in_specs=(placed, placed, placed),
        out_specs=(placed, placed),
        check_vma=False,
    )
```

```python
import math

import jax
import jax.numpy as jnp
from jax import lax
from jax.experimental import pallas as pl
from jax.experimental.pallas import tpu as pltpu
from jax.sharding import Mesh
from jax.sharding import PartitionSpec as P

D = 3584
C = 384
ITERS = 5
BLK = 128

MOMENTUM_COEF = 0.95
NORM_EPS = 1e-07
A_COEF = 3.4445
B_COEF = -4.775
C_COEF = 2.0315
WEIGHT_DECAY = 0.1

f32 = jnp.float32
bf16 = jnp.bfloat16


def dot(a, b):
    return jnp.dot(a, b, preferred_element_type=f32)


def split(value):
    high = value.astype(bf16)
    low = (value - high.astype(f32)).astype(bf16)
    return high, low


def momentum_kernel(place_ref, m_ref, g_ref, nm_ref, *out_refs):
    me = place_ref[1]
    for step, out_ref in enumerate(out_refs):
        index = lax.rem(me + step, len(out_refs))
        new = MOMENTUM_COEF * m_ref[index] + g_ref[index].astype(f32)
        nm_ref[index] = new
        out_ref[...] = new.astype(bf16)


def gram_kernel(place_ref, *refs):
    row_refs, out_refs, stack = refs[:4], refs[4:12], refs[12]
    rows = jnp.concatenate([ref[...] for ref in row_refs], axis=0)

    def cross(i, j0, j1):
        return lax.dot_general(
            rows[:, i * BLK : (i + 1) * BLK],
            rows[:, j0 * BLK : j1 * BLK],
            (((0,), (0,)), ((), ())),
            preferred_element_type=f32,
        )

    def put(j, block):
        stack[j * BLK : (j + 1) * BLK] = block

    @pl.when(place_ref[2] == 0)
    def _():
        top = cross(0, 0, 3)
        for j in range(3):
            put(j, top[:, j * BLK : (j + 1) * BLK])

    @pl.when(place_ref[2] != 0)
    def _():
        middle = cross(1, 1, 3)
        put(0, middle[:, :BLK])
        put(1, middle[:, BLK:])
        put(2, cross(2, 2, 3))

    size = out_refs[0].shape[0]
    for step, out_ref in enumerate(out_refs):
        index = lax.rem(place_ref[0] + step, len(out_refs))
        out_ref[...] = stack[pl.ds(pl.multiple_of(index * size, size), size)]


def chain_kernel(place_ref, own_ref, other_ref, *refs):
    row_refs, out_refs, stack = refs[:4], refs[4:8], refs[8]
    core = place_ref[2]
    parts = 8
    size = own_ref.shape[0] // parts
    for source, ref in ((core, own_ref), (1 - core, other_ref)):
        for step in range(parts):
            index = lax.rem(place_ref[0] + parts - step, parts)
            stack[source, pl.ds(pl.multiple_of(index * size, size), size)] = ref[
                step * size : (step + 1) * size
            ]
    b = [stack[i // 3, (i % 3) * BLK : (i % 3 + 1) * BLK] for i in range(6)]
    gram = jnp.concatenate(
        [
            jnp.concatenate([b[0], b[1], b[2]], axis=1),
            jnp.concatenate([b[1].T, b[3], b[4]], axis=1),
            jnp.concatenate([b[2].T, b[4].T, b[5]], axis=1),
        ],
        axis=0,
    )
    row = lax.broadcasted_iota(jnp.int32, (BLK, BLK), 0)
    col = lax.broadcasted_iota(jnp.int32, (BLK, BLK), 1)
    diagonal = jnp.where(row == col, b[0] + b[3] + b[5], 0.0)
    total = jnp.sum(jnp.sum(diagonal, axis=1, keepdims=True), axis=0, keepdims=True)
    norm = jnp.sqrt(total) + NORM_EPS
    gram = gram / (norm * norm)
    rows = jnp.concatenate([ref[...] for ref in row_refs], axis=0)
    iterate = (rows.astype(f32) / norm).astype(bf16)
    for iteration in range(ITERS):
        g = gram.astype(bf16)
        poly = (B_COEF * g.astype(f32) + C_COEF * dot(g, g)).astype(bf16)
        iterate = (A_COEF * iterate.astype(f32) + dot(iterate, poly)).astype(bf16)
        if iteration < ITERS - 1:
            high, low = split(gram)
            half = A_COEF * gram + (dot(poly, high) + dot(poly, low))
            high, low = split(half)
            gram = A_COEF * half + (dot(high, poly) + dot(low, poly))
    count = out_refs[0].shape[0]
    for i, out_ref in enumerate(out_refs):
        out_ref[...] = iterate[i * count : (i + 1) * count]


def update_kernel(place_ref, w_ref, *refs):
    x_refs, out_ref = refs[:-1], refs[-1]
    scale = 0.2 * math.sqrt(max(D, C))
    for step, x_ref in enumerate(x_refs):
        index = lax.rem(place_ref[1] + step, len(x_refs))
        out_ref[index] = (
            scale * x_ref[...].astype(f32) + WEIGHT_DECAY * w_ref[index].astype(f32)
        ).astype(bf16)


def send(value, axis, size, step):
    return lax.ppermute(value, axis, [(i, (i + step) % size) for i in range(size)])


def call(kernel, inputs, outputs, scratch=()):
    vmem = pl.BlockSpec(memory_space=pltpu.VMEM)
    return pl.pallas_call(
        kernel,
        out_shape=outputs,
        in_specs=[pl.BlockSpec(memory_space=pltpu.SMEM)] + [vmem] * (len(inputs) - 1),
        out_specs=jax.tree.map(lambda _: vmem, outputs),
        scratch_shapes=scratch,
    )(*inputs)


def body(momentum, gradient, weight):
    mats, rows, _ = momentum.shape
    ny, nx = 8, 4
    shape = jax.ShapeDtypeStruct
    place = jnp.stack([lax.axis_index(a) for a in ("y", "x", "replica")]).astype(jnp.int32)
    piece = shape((rows, C), bf16)
    new_momentum, *out = call(
        momentum_kernel,
        [place, momentum, gradient],
        [shape(momentum.shape, f32)] + [piece] * nx,
    )
    owned = [out[0]] + [send(out[s], "x", nx, s) for s in range(1, nx)]
    size = 3 * BLK // ny
    chunks = call(
        gram_kernel,
        [place] + owned,
        [shape((size, BLK), f32)] * ny,
        [pltpu.VMEM((3 * BLK, BLK), f32)],
    )
    arrived = [chunks[0]] + [send(chunks[s], "y", ny, s) for s in range(1, ny)]
    total = sum(arrived[1:], arrived[0])
    half = jnp.concatenate([total] + [send(total, "y", ny, s) for s in range(1, ny)], axis=0)
    other = send(half, "replica", 2, 1)
    final = call(
        chain_kernel,
        [place, half, other] + owned,
        [piece] * nx,
        [pltpu.VMEM((2, 3 * BLK, BLK), f32)],
    )
    back = [final[0]] + [send(final[s], "x", nx, -s) for s in range(1, nx)]
    update = call(update_kernel, [place, weight] + back, shape(weight.shape, bf16))
    return (new_momentum, update)


def solution(mesh):
    devices = mesh.devices.reshape(8, 4, 8, 2)
    grid = Mesh(devices, ("y", "x", "expert", "replica"))
    placed = P("expert", ("y", "x"), None)
    return jax.shard_map(
        body,
        mesh=grid,
        in_specs=(placed, placed, placed),
        out_specs=(placed, placed),
        check_vma=False,
    )
```

```python
import math

import jax
import jax.numpy as jnp
from jax import lax
from jax.experimental import pallas as pl
from jax.experimental.pallas import tpu as pltpu
from jax.sharding import Mesh
from jax.sharding import PartitionSpec as P

D = 3584
C = 384
ITERS = 5
BLK = 128

MOMENTUM_COEF = 0.95
NORM_EPS = 1e-07
A_COEF = 3.4445
B_COEF = -4.775
C_COEF = 2.0315
WEIGHT_DECAY = 0.1

f32 = jnp.float32
bf16 = jnp.bfloat16


def dot(a, b):
    return jnp.dot(a, b, preferred_element_type=f32)


def split(value):
    high = value.astype(bf16)
    low = (value - high.astype(f32)).astype(bf16)
    return high, low


def chain_kernel(blocks_ref, own_ref, got_ref, own_out_ref, got_out_ref):
    b = [blocks_ref[i * BLK : (i + 1) * BLK] for i in range(6)]
    gram = jnp.concatenate(
        [
            jnp.concatenate([b[0], b[1], b[2]], axis=1),
            jnp.concatenate([b[1].T, b[3], b[4]], axis=1),
            jnp.concatenate([b[2].T, b[4].T, b[5]], axis=1),
        ],
        axis=0,
    )
    row = lax.broadcasted_iota(jnp.int32, (BLK, BLK), 0)
    col = lax.broadcasted_iota(jnp.int32, (BLK, BLK), 1)
    diagonal = jnp.where(row == col, b[0] + b[3] + b[5], 0.0)
    total = jnp.sum(jnp.sum(diagonal, axis=1, keepdims=True), axis=0, keepdims=True)
    norm = jnp.sqrt(total) + NORM_EPS
    gram = gram / (norm * norm)
    rows = jnp.concatenate([own_ref[...], got_ref[...]], axis=0)
    iterate = (rows.astype(f32) / norm).astype(bf16)
    for iteration in range(ITERS):
        g = gram.astype(bf16)
        poly = (B_COEF * g.astype(f32) + C_COEF * dot(g, g)).astype(bf16)
        iterate = (A_COEF * iterate.astype(f32) + dot(iterate, poly)).astype(bf16)
        if iteration < ITERS - 1:
            high, low = split(gram)
            half = A_COEF * gram + (dot(poly, high) + dot(poly, low))
            high, low = split(half)
            gram = A_COEF * half + (dot(high, poly) + dot(low, poly))
    count = own_ref.shape[0]
    own_out_ref[...] = iterate[:count]
    got_out_ref[...] = iterate[count:]


def packed_gram(rows):
    gram = lax.dot_general(rows, rows, (((0,), (0,)), ((), ())), preferred_element_type=f32)
    blocks = [
        gram[i * BLK : (i + 1) * BLK, j * BLK : (j + 1) * BLK]
        for i in range(3)
        for j in range(i, 3)
    ]
    return jnp.concatenate(blocks, axis=0)


def body(momentum, gradient, weight):
    mats, rows, _ = momentum.shape
    group = ("y", "pair")
    members = 16
    side = lax.axis_index("side")
    first = 2 * lax.axis_index("replica")

    def rounded(index):
        m = lax.dynamic_index_in_dim(momentum, index, 0, keepdims=False)
        g = lax.dynamic_index_in_dim(gradient, index, 0, keepdims=False)
        return (MOMENTUM_COEF * m + g.astype(f32)).astype(bf16)

    got = lax.ppermute(rounded(first + 1 - side), "side", [(0, 1), (1, 0)])
    own = rounded(first + side)
    new_momentum = MOMENTUM_COEF * momentum + gradient.astype(f32)
    partial = packed_gram(jnp.concatenate([own, got], axis=0))
    size = partial.shape[0] // members
    pieces = partial.reshape(members, size, BLK)
    pieces = lax.all_to_all(pieces, group, split_axis=0, concat_axis=0, tiled=True)
    mine = jnp.broadcast_to(jnp.sum(pieces, axis=0)[None], pieces.shape)
    blocks = lax.all_to_all(mine, group, split_axis=0, concat_axis=0, tiled=True)
    piece = jax.ShapeDtypeStruct((rows, C), bf16)
    own, got = pl.pallas_call(chain_kernel, out_shape=(piece, piece))(
        blocks.reshape(partial.shape), own, got
    )
    got = lax.ppermute(got, "side", [(0, 1), (1, 0)])
    both = jnp.where(side == 0, jnp.stack([own, got]), jnp.stack([got, own]))
    finished = lax.all_gather(both, "replica", axis=0, tiled=True)
    scale = 0.2 * math.sqrt(max(D, C))
    update = (scale * finished.astype(f32) + WEIGHT_DECAY * weight.astype(f32)).astype(bf16)
    return (new_momentum, update)


def solution(mesh):
    devices = mesh.devices.reshape(8, 2, 2, 8, 2)
    grid = Mesh(devices, ("y", "pair", "side", "expert", "replica"))
    placed = P("expert", ("y", "pair", "side"), None)
    return jax.shard_map(
        body,
        mesh=grid,
        in_specs=(placed, placed, placed),
        out_specs=(placed, placed),
        check_vma=False,
    )
```

```python
import math

import jax
import jax.numpy as jnp
from jax import lax
from jax.experimental import pallas as pl
from jax.experimental.pallas import tpu as pltpu
from jax.sharding import Mesh
from jax.sharding import PartitionSpec as P

D = 3584
C = 384
ITERS = 5
BLK = 128

MOMENTUM_COEF = 0.95
NORM_EPS = 1e-07
A_COEF = 3.4445
B_COEF = -4.775
C_COEF = 2.0315
WEIGHT_DECAY = 0.1

f32 = jnp.float32
bf16 = jnp.bfloat16


def dot(a, b):
    return jnp.dot(a, b, preferred_element_type=f32)


def split(value):
    high = value.astype(bf16)
    low = (value - high.astype(f32)).astype(bf16)
    return high, low


def chain_kernel(blocks_ref, own_ref, got_ref, own_out_ref, got_out_ref):
    b = [blocks_ref[i * BLK : (i + 1) * BLK] for i in range(6)]
    gram = jnp.concatenate(
        [
            jnp.concatenate([b[0], b[1], b[2]], axis=1),
            jnp.concatenate([b[1].T, b[3], b[4]], axis=1),
            jnp.concatenate([b[2].T, b[4].T, b[5]], axis=1),
        ],
        axis=0,
    )
    row = lax.broadcasted_iota(jnp.int32, (BLK, BLK), 0)
    col = lax.broadcasted_iota(jnp.int32, (BLK, BLK), 1)
    diagonal = jnp.where(row == col, b[0] + b[3] + b[5], 0.0)
    total = jnp.sum(jnp.sum(diagonal, axis=1, keepdims=True), axis=0, keepdims=True)
    norm = jnp.sqrt(total) + NORM_EPS
    gram = gram / (norm * norm)
    rows = jnp.concatenate([own_ref[...], got_ref[...]], axis=0)
    iterate = (rows.astype(f32) / norm).astype(bf16)
    for iteration in range(ITERS):
        g = gram.astype(bf16)
        poly = (B_COEF * g.astype(f32) + C_COEF * dot(g, g)).astype(bf16)
        iterate = (A_COEF * iterate.astype(f32) + dot(iterate, poly)).astype(bf16)
        if iteration < ITERS - 1:
            high, low = split(gram)
            wide = jnp.concatenate([poly, poly], axis=1)
            half = A_COEF * gram + dot(wide, jnp.concatenate([high, low], axis=0))
            high, low = split(half)
            tall = jnp.concatenate([poly, poly], axis=0)
            gram = A_COEF * half + dot(jnp.concatenate([high, low], axis=1), tall)
    count = own_ref.shape[0]
    own_out_ref[...] = iterate[:count]
    got_out_ref[...] = iterate[count:]


def pack_kernel(gram_ref, out_ref, sems):
    copies = []
    for i in range(3):
        for j in range(i, 3):
            k = len(copies)
            copies.append(
                pltpu.make_async_copy(
                    gram_ref.at[pl.ds(i * BLK, BLK), pl.ds(j * BLK, BLK)],
                    out_ref.at[pl.ds(k * BLK, BLK)],
                    sems.at[k],
                )
            )
    for copy in copies:
        copy.start()
    for copy in copies:
        copy.wait()


def packed_gram(rows):
    gram = lax.dot_general(rows, rows, (((0,), (0,)), ((), ())), preferred_element_type=f32)
    return pl.pallas_call(
        pack_kernel,
        out_shape=jax.ShapeDtypeStruct((6 * BLK, BLK), f32),
        out_specs=pl.BlockSpec(memory_space=pltpu.HBM),
        scratch_shapes=[pltpu.SemaphoreType.DMA((6,))],
    )(gram)


def sum_kernel(pieces_ref, out_ref, total, sems):
    total[...] = jnp.sum(pieces_ref[...], axis=0)
    copies = [
        pltpu.make_async_copy(total, out_ref.at[k], sems.at[k])
        for k in range(out_ref.shape[0])
    ]
    for copy in copies:
        copy.start()
    for copy in copies:
        copy.wait()


def summed_copies(pieces):
    return pl.pallas_call(
        sum_kernel,
        out_shape=jax.ShapeDtypeStruct(pieces.shape, f32),
        out_specs=pl.BlockSpec(memory_space=pltpu.HBM),
        scratch_shapes=[
            pltpu.VMEM(pieces.shape[1:], f32),
            pltpu.SemaphoreType.DMA((pieces.shape[0],)),
        ],
    )(pieces)


def body(momentum, gradient, weight):
    mats, rows, _ = momentum.shape
    group = ("y", "pair")
    members = 16
    side = lax.axis_index("side")
    first = 2 * lax.axis_index("replica")

    def rounded(index):
        m = lax.dynamic_index_in_dim(momentum, index, 0, keepdims=False)
        g = lax.dynamic_index_in_dim(gradient, index, 0, keepdims=False)
        return (MOMENTUM_COEF * m + g.astype(f32)).astype(bf16)

    got = lax.ppermute(rounded(first + 1 - side), "side", [(0, 1), (1, 0)])
    own = rounded(first + side)
    new_momentum = MOMENTUM_COEF * momentum + gradient.astype(f32)
    partial = packed_gram(jnp.concatenate([own, got], axis=0))
    size = partial.shape[0] // members
    pieces = partial.reshape(members, size, BLK)
    pieces = lax.all_to_all(pieces, group, split_axis=0, concat_axis=0, tiled=True)
    blocks = lax.all_to_all(summed_copies(pieces), group, split_axis=0, concat_axis=0, tiled=True)
    piece = jax.ShapeDtypeStruct((rows, C), bf16)
    own, got = pl.pallas_call(chain_kernel, out_shape=(piece, piece))(
        blocks.reshape(partial.shape), own, got
    )
    got = lax.ppermute(got, "side", [(0, 1), (1, 0)])
    both = jnp.where(side == 0, jnp.stack([own, got]), jnp.stack([got, own]))
    finished = lax.all_gather(both, "replica", axis=0, tiled=True)
    scale = 0.2 * math.sqrt(max(D, C))
    update = (scale * finished.astype(f32) + WEIGHT_DECAY * weight.astype(f32)).astype(bf16)
    return (new_momentum, update)


def solution(mesh):
    devices = mesh.devices.reshape(8, 2, 2, 8, 2)
    grid = Mesh(devices, ("y", "pair", "side", "expert", "replica"))
    placed = P("expert", ("y", "pair", "side"), None)
    return jax.shard_map(
        body,
        mesh=grid,
        in_specs=(placed, placed, placed),
        out_specs=(placed, placed),
        check_vma=False,
    )
```

```python
import math

import jax
import jax.numpy as jnp
from jax import lax
from jax.experimental import pallas as pl
from jax.experimental.pallas import tpu as pltpu
from jax.sharding import Mesh
from jax.sharding import PartitionSpec as P

D = 3584
C = 384
ITERS = 5
BLK = 128

MOMENTUM_COEF = 0.95
NORM_EPS = 1e-07
A_COEF = 3.4445
B_COEF = -4.775
C_COEF = 2.0315
WEIGHT_DECAY = 0.1

f32 = jnp.float32
bf16 = jnp.bfloat16


def dot(a, b):
    return jnp.dot(a, b, preferred_element_type=f32)


def split(value):
    high = value.astype(bf16)
    low = (value - high.astype(f32)).astype(bf16)
    return high, low


def indices():
    row = lax.broadcasted_iota(jnp.int32, (BLK, BLK), 0)
    col = lax.broadcasted_iota(jnp.int32, (BLK, BLK), 1)
    return row, col


def pack(gram):
    row, col = indices()

    def block(i, j):
        return gram[i * BLK : (i + 1) * BLK, j * BLK : (j + 1) * BLK]

    middle = block(1, 1)
    diagonal = jnp.sum(jnp.where(row == col, middle, 0.0), axis=0, keepdims=True)
    last = diagonal[:, BLK - 1 :]
    first = jnp.where(row <= col, block(0, 0), middle)
    spare = jnp.where(row == BLK - 1, diagonal, last)
    second = jnp.where(row <= col, block(2, 2), spare)
    return jnp.concatenate([first, block(0, 1), block(0, 2), block(1, 2), second], axis=0)


def unpack(ref):
    row, col = indices()
    first, b01, b02, b12, second = [ref[i * BLK : (i + 1) * BLK] for i in range(5)]
    first_t, second_t = first.T, second.T
    b00 = jnp.where(row <= col, first, first_t)
    b22 = jnp.where(row <= col, second, second_t)
    diagonal = jnp.where(
        col[:1] < BLK - 1, second[BLK - 1 :], jnp.broadcast_to(second[BLK - 2 : BLK - 1, :1], (1, BLK))
    )
    b11 = jnp.where(row == col, diagonal, jnp.where(row > col, first, first_t))
    trace = jnp.where(row == col, b00 + b11 + b22, 0.0)
    gram = jnp.concatenate(
        [
            jnp.concatenate([b00, b01, b02], axis=1),
            jnp.concatenate([b01.T, b11, b12], axis=1),
            jnp.concatenate([b02.T, b12.T, b22], axis=1),
        ],
        axis=0,
    )
    return gram, jnp.sum(jnp.sum(trace, axis=1, keepdims=True), axis=0, keepdims=True)


def chain_kernel(packed_ref, rows_ref, out_ref):
    gram, total = unpack(packed_ref)
    norm = jnp.sqrt(total) + NORM_EPS
    gram = gram / (norm * norm)
    iterate = (rows_ref[...].astype(f32) / norm).astype(bf16)
    for iteration in range(ITERS):
        g = gram.astype(bf16)
        poly = (B_COEF * g.astype(f32) + C_COEF * dot(g, g)).astype(bf16)
        iterate = (A_COEF * iterate.astype(f32) + dot(iterate, poly)).astype(bf16)
        if iteration < ITERS - 1:
            high, low = split(gram)
            wide = jnp.concatenate([poly, poly], axis=1)
            half = A_COEF * gram + dot(wide, jnp.concatenate([high, low], axis=0))
            high, low = split(half)
            tall = jnp.concatenate([poly, poly], axis=0)
            gram = A_COEF * half + dot(jnp.concatenate([high, low], axis=1), tall)
    out_ref[...] = iterate


def body(momentum, gradient, weight):
    mats, rows, _ = momentum.shape
    members = 8
    new_momentum = MOMENTUM_COEF * momentum + gradient.astype(f32)
    rounded = new_momentum.astype(bf16)
    owned = lax.all_to_all(rounded, "x", split_axis=0, concat_axis=0, tiled=True)
    owned = owned.reshape(mats * rows, C)
    gram = lax.dot_general(owned, owned, (((0,), (0,)), ((), ())), preferred_element_type=f32)
    packed = pack(gram)
    count = packed.shape[0] // 2
    packed = lax.dynamic_slice_in_dim(packed, lax.axis_index("replica") * count, count, 0)
    pieces = packed.reshape(members, count // members, BLK)
    pieces = lax.all_to_all(pieces, "y", split_axis=0, concat_axis=0, tiled=True)
    mine = jnp.broadcast_to(jnp.sum(pieces, axis=0)[None], pieces.shape)
    half = lax.all_to_all(mine, "y", split_axis=0, concat_axis=0, tiled=True)
    packed = lax.all_gather(half.reshape(count, BLK), "replica", axis=0, tiled=True)
    final = pl.pallas_call(
        chain_kernel, out_shape=jax.ShapeDtypeStruct((mats * rows, C), bf16)
    )(packed, owned)
    back = final.reshape(mats, rows, C)
    finished = lax.all_to_all(back, "x", split_axis=0, concat_axis=0, tiled=True)
    scale = 0.2 * math.sqrt(max(D, C))
    update = (scale * finished.astype(f32) + WEIGHT_DECAY * weight.astype(f32)).astype(bf16)
    return (new_momentum, update)


def solution(mesh):
    devices = mesh.devices.reshape(8, 4, 8, 2)
    grid = Mesh(devices, ("y", "x", "expert", "replica"))
    placed = P("expert", ("y", "x"), None)
    return jax.shard_map(
        body,
        mesh=grid,
        in_specs=(placed, placed, placed),
        out_specs=(placed, placed),
        check_vma=False,
    )
```

```python
import math

import jax
import jax.numpy as jnp
from jax import lax
from jax.experimental import pallas as pl
from jax.experimental.pallas import tpu as pltpu
from jax.sharding import Mesh
from jax.sharding import PartitionSpec as P

D = 3584
C = 384
ITERS = 5
BLK = 128

MOMENTUM_COEF = 0.95
NORM_EPS = 1e-07
A_COEF = 3.4445
B_COEF = -4.775
C_COEF = 2.0315
WEIGHT_DECAY = 0.1

f32 = jnp.float32
bf16 = jnp.bfloat16


def dot(a, b):
    return jnp.dot(a, b, preferred_element_type=f32)


def split(value):
    high = value.astype(bf16)
    low = (value - high.astype(f32)).astype(bf16)
    return high, low


def chain_kernel(blocks_ref, own_ref, got_ref, own_out_ref, got_out_ref):
    b = [blocks_ref[i * BLK : (i + 1) * BLK] for i in range(6)]
    gram = jnp.concatenate(
        [
            jnp.concatenate([b[0], b[1], b[2]], axis=1),
            jnp.concatenate([b[1].T, b[3], b[4]], axis=1),
            jnp.concatenate([b[2].T, b[4].T, b[5]], axis=1),
        ],
        axis=0,
    )
    row = lax.broadcasted_iota(jnp.int32, (BLK, BLK), 0)
    col = lax.broadcasted_iota(jnp.int32, (BLK, BLK), 1)
    diagonal = jnp.where(row == col, b[0] + b[3] + b[5], 0.0)
    total = jnp.sum(jnp.sum(diagonal, axis=1, keepdims=True), axis=0, keepdims=True)
    norm = jnp.sqrt(total) + NORM_EPS
    gram = gram / (norm * norm)
    rows = jnp.concatenate([own_ref[...], got_ref[...]], axis=0)
    iterate = (rows.astype(f32) / norm).astype(bf16)
    for iteration in range(ITERS):
        g = gram.astype(bf16)
        poly = (B_COEF * g.astype(f32) + C_COEF * dot(g, g)).astype(bf16)
        iterate = (A_COEF * iterate.astype(f32) + dot(iterate, poly)).astype(bf16)
        if iteration < ITERS - 1:
            high, low = split(gram)
            wide = jnp.concatenate([poly, poly], axis=1)
            half = A_COEF * gram + dot(wide, jnp.concatenate([high, low], axis=0))
            high, low = split(half)
            tall = jnp.concatenate([poly, poly], axis=0)
            gram = A_COEF * half + dot(jnp.concatenate([high, low], axis=1), tall)
    count = own_ref.shape[0]
    own_out_ref[...] = iterate[:count]
    got_out_ref[...] = iterate[count:]


def packed_gram(rows):
    gram = lax.dot_general(rows, rows, (((0,), (0,)), ((), ())), preferred_element_type=f32)
    blocks = [
        gram[i * BLK : (i + 1) * BLK, j * BLK : (j + 1) * BLK]
        for i in range(3)
        for j in range(i, 3)
    ]
    return jnp.concatenate(blocks, axis=0)


def body(momentum, gradient, weight):
    mats, rows, _ = momentum.shape
    members = 8
    side = lax.axis_index("side")
    first = 2 * lax.axis_index("replica")

    def rounded(index):
        m = lax.dynamic_index_in_dim(momentum, index, 0, keepdims=False)
        g = lax.dynamic_index_in_dim(gradient, index, 0, keepdims=False)
        return (MOMENTUM_COEF * m + g.astype(f32)).astype(bf16)

    got = lax.ppermute(rounded(first + 1 - side), "side", [(0, 1), (1, 0)])
    own = rounded(first + side)
    new_momentum = MOMENTUM_COEF * momentum + gradient.astype(f32)
    partial = packed_gram(jnp.concatenate([own, got], axis=0))
    size = partial.shape[0] // members
    pieces = partial.reshape(members, size, BLK)
    pieces = lax.all_to_all(pieces, "y", split_axis=0, concat_axis=0, tiled=True)
    mine = lax.all_gather(jnp.sum(pieces, axis=0), "pair", axis=0, tiled=False)
    mine = jnp.broadcast_to((mine[0] + mine[1])[None], pieces.shape)
    blocks = lax.all_to_all(mine, "y", split_axis=0, concat_axis=0, tiled=True)
    piece = jax.ShapeDtypeStruct((rows, C), bf16)
    own, got = pl.pallas_call(chain_kernel, out_shape=(piece, piece))(
        blocks.reshape(partial.shape), own, got
    )
    got = lax.ppermute(got, "side", [(0, 1), (1, 0)])
    both = jnp.where(side == 0, jnp.stack([own, got]), jnp.stack([got, own]))
    finished = lax.all_gather(both, "replica", axis=0, tiled=True)
    scale = 0.2 * math.sqrt(max(D, C))
    update = (scale * finished.astype(f32) + WEIGHT_DECAY * weight.astype(f32)).astype(bf16)
    return (new_momentum, update)


def solution(mesh):
    devices = mesh.devices.reshape(8, 2, 2, 8, 2)
    grid = Mesh(devices, ("y", "pair", "side", "expert", "replica"))
    placed = P("expert", ("y", "pair", "side"), None)
    return jax.shard_map(
        body,
        mesh=grid,
        in_specs=(placed, placed, placed),
        out_specs=(placed, placed),
        check_vma=False,
    )
```

```python
import math

import jax
import jax.numpy as jnp
from jax import lax
from jax.experimental import pallas as pl
from jax.experimental.pallas import tpu as pltpu
from jax.sharding import Mesh
from jax.sharding import PartitionSpec as P

D = 3584
C = 384
ITERS = 5
BLK = 128

MOMENTUM_COEF = 0.95
NORM_EPS = 1e-07
A_COEF = 3.4445
B_COEF = -4.775
C_COEF = 2.0315
WEIGHT_DECAY = 0.1

f32 = jnp.float32
bf16 = jnp.bfloat16


def dot(a, b):
    return jnp.dot(a, b, preferred_element_type=f32)


def split(value):
    high = value.astype(bf16)
    low = (value - high.astype(f32)).astype(bf16)
    return high, low


def chain_kernel(blocks_ref, rows_ref, out_ref):
    b = [blocks_ref[i * BLK : (i + 1) * BLK] for i in range(6)]
    gram = jnp.concatenate(
        [
            jnp.concatenate([b[0], b[1], b[2]], axis=1),
            jnp.concatenate([b[1].T, b[3], b[4]], axis=1),
            jnp.concatenate([b[2].T, b[4].T, b[5]], axis=1),
        ],
        axis=0,
    )
    row = lax.broadcasted_iota(jnp.int32, (BLK, BLK), 0)
    col = lax.broadcasted_iota(jnp.int32, (BLK, BLK), 1)
    diagonal = jnp.where(row == col, b[0] + b[3] + b[5], 0.0)
    total = jnp.sum(jnp.sum(diagonal, axis=1, keepdims=True), axis=0, keepdims=True)
    norm = jnp.sqrt(total) + NORM_EPS
    gram = gram / (norm * norm)
    iterate = (rows_ref[...].astype(f32) / norm).astype(bf16)
    for iteration in range(ITERS):
        g = gram.astype(bf16)
        poly = (B_COEF * g.astype(f32) + C_COEF * dot(g, g)).astype(bf16)
        iterate = (A_COEF * iterate.astype(f32) + dot(iterate, poly)).astype(bf16)
        if iteration < ITERS - 1:
            high, low = split(gram)
            wide = jnp.concatenate([poly, poly], axis=1)
            half = A_COEF * gram + dot(wide, jnp.concatenate([high, low], axis=0))
            high, low = split(half)
            tall = jnp.concatenate([poly, poly], axis=0)
            gram = A_COEF * half + dot(jnp.concatenate([high, low], axis=1), tall)
    out_ref[...] = iterate


def half_gram(rows, core):
    gram = lax.dot_general(rows, rows, (((0,), (0,)), ((), ())), preferred_element_type=f32)

    def stack(pairs):
        return jnp.concatenate(
            [gram[i * BLK : (i + 1) * BLK, j * BLK : (j + 1) * BLK] for i, j in pairs], axis=0
        )

    return jnp.where(
        core == 0, stack([(0, 0), (0, 1), (0, 2)]), stack([(1, 1), (1, 2), (2, 2)])
    )


CORE_PEER = [(2 * x + c, 2 * (x ^ (1 + c)) + c) for x in range(4) for c in range(2)]
FAR_PEER = [(2 * x + c, 2 * (x ^ 3) + c) for x in range(4) for c in range(2)]


def body(momentum, gradient, weight):
    rows = momentum.shape[1]
    part = rows // 2
    members = 8
    x = lax.axis_index("x")
    core = lax.axis_index("replica")

    def rounded(index, start, count):
        m = lax.dynamic_slice(momentum, (index, start, 0), (1, count, C))[0]
        g = lax.dynamic_slice(gradient, (index, start, 0), (1, count, C))[0]
        return (MOMENTUM_COEF * m + g.astype(f32)).astype(bf16)

    def trade(near, far):
        near = lax.ppermute(near, ("x", "replica"), CORE_PEER)
        far = lax.ppermute(far, ("x", "replica"), FAR_PEER)
        return near, far

    near, far = trade(rounded(x ^ (1 + core), 0, rows), rounded(x ^ 3, core * part, part))
    mine = jnp.concatenate([rounded(x, core * part, part), near, far], axis=0)
    new_momentum = MOMENTUM_COEF * momentum + gradient.astype(f32)
    partial = half_gram(lax.all_gather(mine, "replica", axis=0, tiled=True), core)
    pieces = partial.reshape(members, partial.shape[0] // members, BLK)
    pieces = lax.all_to_all(pieces, "y", split_axis=0, concat_axis=0, tiled=True)
    total = jnp.broadcast_to(jnp.sum(pieces, axis=0)[None], pieces.shape)
    half = lax.all_to_all(total, "y", split_axis=0, concat_axis=0, tiled=True)
    blocks = lax.all_gather(half.reshape(partial.shape), "replica", axis=0, tiled=True)
    final = pl.pallas_call(chain_kernel, out_shape=jax.ShapeDtypeStruct(mine.shape, bf16))(
        blocks, mine
    )
    near, far = trade(final[part : part + rows], final[part + rows :])
    mine = jnp.concatenate([final[:part], near, far], axis=0)
    both = lax.all_gather(mine, "replica", axis=0, tiled=False)
    by_distance = jnp.stack(
        [
            both[:, :part].reshape(rows, C),
            both[0, part : part + rows],
            both[1, part : part + rows],
            both[:, part + rows :].reshape(rows, C),
        ]
    )
    finished = jnp.stack(
        [lax.dynamic_index_in_dim(by_distance, x ^ i, 0, keepdims=False) for i in range(4)]
    )
    scale = 0.2 * math.sqrt(max(D, C))
    update = (scale * finished.astype(f32) + WEIGHT_DECAY * weight.astype(f32)).astype(bf16)
    return (new_momentum, update)


def solution(mesh):
    devices = mesh.devices.reshape(8, 4, 8, 2)
    grid = Mesh(devices, ("y", "x", "expert", "replica"))
    placed = P("expert", ("y", "x"), None)
    return jax.shard_map(
        body,
        mesh=grid,
        in_specs=(placed, placed, placed),
        out_specs=(placed, placed),
        check_vma=False,
    )
```

```python
import math

import jax
import jax.numpy as jnp
from jax import lax
from jax.experimental import pallas as pl
from jax.experimental.pallas import tpu as pltpu
from jax.sharding import Mesh
from jax.sharding import PartitionSpec as P

D = 3584
C = 384
ITERS = 5
BLK = 128

MOMENTUM_COEF = 0.95
NORM_EPS = 1e-07
A_COEF = 3.4445
B_COEF = -4.775
C_COEF = 2.0315
WEIGHT_DECAY = 0.1

f32 = jnp.float32
bf16 = jnp.bfloat16


def dot(a, b):
    return jnp.dot(a, b, preferred_element_type=f32)


def split(value):
    high = value.astype(bf16)
    low = (value - high.astype(f32)).astype(bf16)
    return high, low


def chain_kernel(blocks_ref, rows_ref, out_ref):
    b = [blocks_ref[i * BLK : (i + 1) * BLK] for i in range(6)]
    gram = jnp.concatenate(
        [
            jnp.concatenate([b[0], b[1], b[2]], axis=1),
            jnp.concatenate([b[1].T, b[3], b[4]], axis=1),
            jnp.concatenate([b[2].T, b[4].T, b[5]], axis=1),
        ],
        axis=0,
    )
    row = lax.broadcasted_iota(jnp.int32, (BLK, BLK), 0)
    col = lax.broadcasted_iota(jnp.int32, (BLK, BLK), 1)
    diagonal = jnp.where(row == col, b[0] + b[3] + b[5], 0.0)
    total = jnp.sum(jnp.sum(diagonal, axis=1, keepdims=True), axis=0, keepdims=True)
    norm = jnp.sqrt(total) + NORM_EPS
    gram = gram / (norm * norm)
    iterate = (rows_ref[...].astype(f32) / norm).astype(bf16)
    for iteration in range(ITERS):
        g = gram.astype(bf16)
        poly = (B_COEF * g.astype(f32) + C_COEF * dot(g, g)).astype(bf16)
        iterate = (A_COEF * iterate.astype(f32) + dot(iterate, poly)).astype(bf16)
        if iteration < ITERS - 1:
            high, low = split(gram)
            wide = jnp.concatenate([poly, poly], axis=1)
            half = A_COEF * gram + dot(wide, jnp.concatenate([high, low], axis=0))
            high, low = split(half)
            tall = jnp.concatenate([poly, poly], axis=0)
            gram = A_COEF * half + dot(jnp.concatenate([high, low], axis=1), tall)
    out_ref[...] = iterate


def half_gram(rows, half):
    gram = lax.dot_general(rows, rows, (((0,), (0,)), ((), ())), preferred_element_type=f32)

    def stack(pairs):
        return jnp.concatenate(
            [gram[i * BLK : (i + 1) * BLK, j * BLK : (j + 1) * BLK] for i, j in pairs], axis=0
        )

    return jnp.where(
        half == 0, stack([(0, 0), (0, 1), (0, 2)]), stack([(1, 1), (1, 2), (2, 2)])
    )


def body(momentum, gradient, weight):
    rows = momentum.shape[1]
    members = 8
    pair = lax.axis_index("pair")
    side = lax.axis_index("side")
    first = 2 * lax.axis_index("replica")

    m = lax.dynamic_slice_in_dim(momentum, first, 2, 0)
    g = lax.dynamic_slice_in_dim(gradient, first, 2, 0)
    rounded = (MOMENTUM_COEF * m + g.astype(f32)).astype(bf16)
    new_momentum = MOMENTUM_COEF * momentum + gradient.astype(f32)
    sent = jnp.concatenate([rounded, rounded], axis=0)
    owned = lax.all_to_all(sent, ("pair", "side"), split_axis=0, concat_axis=0, tiled=True)
    partial = half_gram(owned.reshape(4 * rows, C), pair)
    mine = lax.dynamic_slice_in_dim(owned, 2 * pair, 2, 0).reshape(2 * rows, C)
    pieces = partial.reshape(members, partial.shape[0] // members, BLK)
    pieces = lax.all_to_all(pieces, "y", split_axis=0, concat_axis=0, tiled=True)
    total = jnp.broadcast_to(jnp.sum(pieces, axis=0)[None], (2 * members,) + pieces.shape[1:])
    blocks = lax.all_to_all(total, ("pair", "y"), split_axis=0, concat_axis=0, tiled=True)
    final = pl.pallas_call(chain_kernel, out_shape=jax.ShapeDtypeStruct(mine.shape, bf16))(
        blocks.reshape(2 * partial.shape[0], BLK), mine
    )
    final = final.reshape(2, rows, C)
    got = lax.ppermute(
        lax.dynamic_index_in_dim(final, 1 - side, 0, keepdims=False), "side", [(0, 1), (1, 0)]
    )
    own = lax.dynamic_index_in_dim(final, side, 0, keepdims=False)
    both = jnp.where(side == 0, jnp.stack([own, got]), jnp.stack([got, own]))
    finished = lax.all_gather(both, "replica", axis=0, tiled=True)
    scale = 0.2 * math.sqrt(max(D, C))
    update = (scale * finished.astype(f32) + WEIGHT_DECAY * weight.astype(f32)).astype(bf16)
    return (new_momentum, update)


def solution(mesh):
    devices = mesh.devices.reshape(8, 2, 2, 8, 2)
    grid = Mesh(devices, ("y", "pair", "side", "expert", "replica"))
    placed = P("expert", ("y", "pair", "side"), None)
    return jax.shard_map(
        body,
        mesh=grid,
        in_specs=(placed, placed, placed),
        out_specs=(placed, placed),
        check_vma=False,
    )
```

```python
import math

import jax
import jax.numpy as jnp
from jax import lax
from jax.experimental import pallas as pl
from jax.experimental.pallas import tpu as pltpu
from jax.sharding import Mesh
from jax.sharding import PartitionSpec as P

D = 3584
C = 384
ITERS = 5
BLK = 128

MOMENTUM_COEF = 0.95
NORM_EPS = 1e-07
A_COEF = 3.4445
B_COEF = -4.775
C_COEF = 2.0315
WEIGHT_DECAY = 0.1

f32 = jnp.float32
bf16 = jnp.bfloat16


def dot(a, b):
    return jnp.dot(a, b, preferred_element_type=f32)


def split(value):
    high = value.astype(bf16)
    low = (value - high.astype(f32)).astype(bf16)
    return high, low


def indices():
    row = lax.broadcasted_iota(jnp.int32, (BLK, BLK), 0)
    col = lax.broadcasted_iota(jnp.int32, (BLK, BLK), 1)
    return row, col


def packed_half(rows, half):
    gram = lax.dot_general(rows, rows, (((0,), (0,)), ((), ())), preferred_element_type=f32)
    row, col = indices()

    def block(i, j):
        return lax.slice(gram, (i, j), (i + BLK, j + BLK))

    first = jnp.where(row <= col, block(0, 0), block(BLK, BLK))
    corner = (row == BLK - 1) & (col == 0)
    spare = jnp.where(corner, block(1, BLK), block(BLK, BLK + 1))
    last = jnp.where(row <= col, block(2 * BLK, 2 * BLK), spare)
    split_block = block(0, 2 * BLK)
    return jnp.where(
        half == 0,
        jnp.concatenate([first, block(0, BLK), split_block[: BLK // 2]], axis=0),
        jnp.concatenate([split_block[BLK // 2 :], block(BLK, 2 * BLK), last], axis=0),
    )


def unpack(ref):
    row, col = indices()
    first, b01, b02, b12, last = [ref[i * BLK : (i + 1) * BLK] for i in range(5)]
    first_t, last_t = first.T, last.T
    b00 = jnp.where(row <= col, first, first_t)
    b22 = jnp.where(row <= col, last, last_t)
    corner = jnp.broadcast_to(last[BLK - 1 :, :1], (BLK, BLK))
    diagonal = jnp.where(row == 0, corner, pltpu.roll(last, 1, 1))
    b11 = jnp.where(row == col, diagonal, jnp.where(row > col, first, first_t))
    trace = jnp.where(row == col, b00 + b11 + b22, 0.0)
    gram = jnp.concatenate(
        [
            jnp.concatenate([b00, b01, b02], axis=1),
            jnp.concatenate([b01.T, b11, b12], axis=1),
            jnp.concatenate([b02.T, b12.T, b22], axis=1),
        ],
        axis=0,
    )
    return gram, jnp.sum(jnp.sum(trace, axis=1, keepdims=True), axis=0, keepdims=True)


def chain_kernel(packed_ref, own_ref, got_ref, own_out_ref, got_out_ref):
    gram, total = unpack(packed_ref)
    norm = jnp.sqrt(total) + NORM_EPS
    gram = gram / (norm * norm)
    rows = jnp.concatenate([own_ref[...], got_ref[...]], axis=0)
    iterate = (rows.astype(f32) / norm).astype(bf16)
    for iteration in range(ITERS):
        g = gram.astype(bf16)
        poly = (B_COEF * g.astype(f32) + C_COEF * dot(g, g)).astype(bf16)
        iterate = (A_COEF * iterate.astype(f32) + dot(iterate, poly)).astype(bf16)
        if iteration < ITERS - 1:
            high, low = split(gram)
            wide = jnp.concatenate([poly, poly], axis=1)
            half = A_COEF * gram + dot(wide, jnp.concatenate([high, low], axis=0))
            high, low = split(half)
            tall = jnp.concatenate([poly, poly], axis=0)
            gram = A_COEF * half + dot(jnp.concatenate([high, low], axis=1), tall)
    count = own_ref.shape[0]
    own_out_ref[...] = iterate[:count]
    got_out_ref[...] = iterate[count:]


def body(momentum, gradient, weight):
    rows = momentum.shape[1]
    members = 8
    pair = lax.axis_index("pair")
    side = lax.axis_index("side")
    first = 2 * lax.axis_index("replica")

    m = lax.dynamic_slice_in_dim(momentum, first, 2, 0)
    g = lax.dynamic_slice_in_dim(gradient, first, 2, 0)
    rounded = (MOMENTUM_COEF * m + g.astype(f32)).astype(bf16)
    new_momentum = MOMENTUM_COEF * momentum + gradient.astype(f32)
    sent = jnp.broadcast_to(rounded[None], (2, 2, rows, C)).reshape(4, rows, C)
    owned = lax.all_to_all(sent, ("pair", "side"), split_axis=0, concat_axis=0, tiled=True)
    partial = packed_half(owned.reshape(4 * rows, C), pair)
    own = lax.dynamic_index_in_dim(owned, 2 * pair + side, 0, keepdims=False)
    got = lax.dynamic_index_in_dim(owned, 2 * pair + 1 - side, 0, keepdims=False)
    pieces = partial.reshape(members, partial.shape[0] // members, BLK)
    pieces = lax.all_to_all(pieces, "y", split_axis=0, concat_axis=0, tiled=True)
    total = jnp.broadcast_to(jnp.sum(pieces, axis=0)[None], (2 * members,) + pieces.shape[1:])
    packed = lax.all_to_all(total, ("pair", "y"), split_axis=0, concat_axis=0, tiled=True)
    piece = jax.ShapeDtypeStruct((rows, C), bf16)
    own, got = pl.pallas_call(chain_kernel, out_shape=(piece, piece))(
        packed.reshape(2 * partial.shape[0], BLK), own, got
    )
    got = lax.ppermute(got, "side", [(0, 1), (1, 0)])
    both = jnp.where(side == 0, jnp.stack([own, got]), jnp.stack([got, own]))
    finished = lax.all_gather(both, "replica", axis=0, tiled=True)
    scale = 0.2 * math.sqrt(max(D, C))
    update = (scale * finished.astype(f32) + WEIGHT_DECAY * weight.astype(f32)).astype(bf16)
    return (new_momentum, update)


def solution(mesh):
    devices = mesh.devices.reshape(8, 2, 2, 8, 2)
    grid = Mesh(devices, ("y", "pair", "side", "expert", "replica"))
    placed = P("expert", ("y", "pair", "side"), None)
    return jax.shard_map(
        body,
        mesh=grid,
        in_specs=(placed, placed, placed),
        out_specs=(placed, placed),
        check_vma=False,
    )
```

```python
import math

import jax
import jax.numpy as jnp
from jax import lax
from jax.experimental import pallas as pl
from jax.experimental.pallas import tpu as pltpu
from jax.sharding import Mesh
from jax.sharding import PartitionSpec as P

D = 3584
C = 384
ITERS = 5
BLK = 128

MOMENTUM_COEF = 0.95
NORM_EPS = 1e-07
A_COEF = 3.4445
B_COEF = -4.775
C_COEF = 2.0315
WEIGHT_DECAY = 0.1

f32 = jnp.float32
bf16 = jnp.bfloat16


def dot(a, b):
    return jnp.dot(a, b, preferred_element_type=f32)


def split(value):
    high = value.astype(bf16)
    low = (value - high.astype(f32)).astype(bf16)
    return high, low


def indices():
    row = lax.broadcasted_iota(jnp.int32, (BLK, BLK), 0)
    col = lax.broadcasted_iota(jnp.int32, (BLK, BLK), 1)
    return row, col


def packed_half(rows, half):
    gram = lax.dot_general(rows, rows, (((0,), (0,)), ((), ())), preferred_element_type=f32)
    row, col = indices()

    def block(i, j):
        return lax.slice(gram, (i, j), (i + BLK, j + BLK))

    first = jnp.where(row <= col, block(0, 0), block(BLK, BLK))
    corner = (row == BLK - 1) & (col == 0)
    spare = jnp.where(corner, block(1, BLK), block(BLK, BLK + 1))
    last = jnp.where(row <= col, block(2 * BLK, 2 * BLK), spare)
    split_block = block(0, 2 * BLK)
    return jnp.where(
        half == 0,
        jnp.concatenate([first, block(0, BLK), split_block[: BLK // 2]], axis=0),
        jnp.concatenate([split_block[BLK // 2 :], block(BLK, 2 * BLK), last], axis=0),
    )


def unpack(ref):
    row, col = indices()
    first, b01, b02, b12, last = [ref[i * BLK : (i + 1) * BLK] for i in range(5)]
    first_t, last_t = first.T, last.T
    b00 = jnp.where(row <= col, first, first_t)
    b22 = jnp.where(row <= col, last, last_t)
    corner = jnp.broadcast_to(last[BLK - 1 :, :1], (BLK, BLK))
    diagonal = jnp.where(row == 0, corner, pltpu.roll(last, 1, 1))
    b11 = jnp.where(row == col, diagonal, jnp.where(row > col, first, first_t))
    trace = jnp.where(row == col, b00 + b11 + b22, 0.0)
    gram = jnp.concatenate(
        [
            jnp.concatenate([b00, b01, b02], axis=1),
            jnp.concatenate([b01.T, b11, b12], axis=1),
            jnp.concatenate([b02.T, b12.T, b22], axis=1),
        ],
        axis=0,
    )
    return gram, jnp.sum(jnp.sum(trace, axis=1, keepdims=True), axis=0, keepdims=True)


def chain_kernel(packed_ref, own_ref, got_ref, own_out_ref, got_out_ref, gram_ref, x_ref):
    count = own_ref.shape[0]
    gram, total = unpack(packed_ref)
    norm = jnp.sqrt(total) + NORM_EPS
    gram_ref[...] = gram / (norm * norm)
    x_ref[:count] = (own_ref[...].astype(f32) / norm).astype(bf16)
    x_ref[count:] = (got_ref[...].astype(f32) / norm).astype(bf16)

    def polynomial():
        g = gram_ref[...].astype(bf16)
        return (B_COEF * g.astype(f32) + C_COEF * dot(g, g)).astype(bf16)

    def advance(poly):
        iterate = x_ref[...]
        return (A_COEF * iterate.astype(f32) + dot(iterate, poly)).astype(bf16)

    def step(iteration, carry):
        poly = polynomial()
        gram = gram_ref[...]
        high, low = split(gram)
        wide = jnp.concatenate([poly, poly], axis=1)
        half = A_COEF * gram + dot(wide, jnp.concatenate([high, low], axis=0))
        high, low = split(half)
        tall = jnp.concatenate([poly, poly], axis=0)
        gram_ref[...] = A_COEF * half + dot(jnp.concatenate([high, low], axis=1), tall)
        x_ref[...] = advance(poly)
        return carry

    lax.fori_loop(0, ITERS - 1, step, 0)
    iterate = advance(polynomial())
    own_out_ref[...] = iterate[:count]
    got_out_ref[...] = iterate[count:]


def body(momentum, gradient, weight):
    rows = momentum.shape[1]
    members = 8
    pair = lax.axis_index("pair")
    side = lax.axis_index("side")
    first = 2 * lax.axis_index("replica")

    m = lax.dynamic_slice_in_dim(momentum, first, 2, 0)
    g = lax.dynamic_slice_in_dim(gradient, first, 2, 0)
    rounded = (MOMENTUM_COEF * m + g.astype(f32)).astype(bf16)
    new_momentum = MOMENTUM_COEF * momentum + gradient.astype(f32)
    sent = jnp.broadcast_to(rounded[None], (2, 2, rows, C)).reshape(4, rows, C)
    owned = lax.all_to_all(sent, ("pair", "side"), split_axis=0, concat_axis=0, tiled=True)
    partial = packed_half(owned.reshape(4 * rows, C), pair)
    own = lax.dynamic_index_in_dim(owned, 2 * pair + side, 0, keepdims=False)
    got = lax.dynamic_index_in_dim(owned, 2 * pair + 1 - side, 0, keepdims=False)
    pieces = partial.reshape(members, partial.shape[0] // members, BLK)
    pieces = lax.all_to_all(pieces, "y", split_axis=0, concat_axis=0, tiled=True)
    total = jnp.broadcast_to(jnp.sum(pieces, axis=0)[None], (2 * members,) + pieces.shape[1:])
    packed = lax.all_to_all(total, ("pair", "y"), split_axis=0, concat_axis=0, tiled=True)
    piece = jax.ShapeDtypeStruct((rows, C), bf16)
    own, got = pl.pallas_call(
        chain_kernel,
        out_shape=(piece, piece),
        scratch_shapes=[pltpu.VMEM((C, C), f32), pltpu.VMEM((2 * rows, C), bf16)],
    )(
        packed.reshape(2 * partial.shape[0], BLK), own, got
    )
    got = lax.ppermute(got, "side", [(0, 1), (1, 0)])
    both = jnp.where(side == 0, jnp.stack([own, got]), jnp.stack([got, own]))
    finished = lax.all_gather(both, "replica", axis=0, tiled=True)
    scale = 0.2 * math.sqrt(max(D, C))
    update = (scale * finished.astype(f32) + WEIGHT_DECAY * weight.astype(f32)).astype(bf16)
    return (new_momentum, update)


def solution(mesh):
    devices = mesh.devices.reshape(8, 2, 2, 8, 2)
    grid = Mesh(devices, ("y", "pair", "side", "expert", "replica"))
    placed = P("expert", ("y", "pair", "side"), None)
    return jax.shard_map(
        body,
        mesh=grid,
        in_specs=(placed, placed, placed),
        out_specs=(placed, placed),
        check_vma=False,
    )
```

```python
import math

import jax
import jax.numpy as jnp
from jax import lax
from jax.sharding import Mesh
from jax.sharding import PartitionSpec as P

D = 3584
C = 384
ITERS = 5
BLK = 128

MOMENTUM_COEF = 0.95
NORM_EPS = 1e-07
A_COEF = 3.4445
B_COEF = -4.775
C_COEF = 2.0315
WEIGHT_DECAY = 0.1

f32 = jnp.float32
bf16 = jnp.bfloat16


def dot(a, b):
    return jnp.dot(a, b, preferred_element_type=f32)


def split(value):
    near = lax.reduce_precision(value, 8, 7)
    return near, near.astype(bf16), (value - near).astype(bf16)


def indices():
    row = lax.broadcasted_iota(jnp.int32, (BLK, BLK), 0)
    col = lax.broadcasted_iota(jnp.int32, (BLK, BLK), 1)
    return row, col


def packed_half(rows, half):
    gram = lax.dot_general(rows, rows, (((0,), (0,)), ((), ())), preferred_element_type=f32)
    row, col = indices()

    def block(i, j):
        return lax.slice(gram, (i, j), (i + BLK, j + BLK))

    first = jnp.where(row <= col, block(0, 0), block(BLK, BLK))
    corner = (row == BLK - 1) & (col == 0)
    spare = jnp.where(corner, block(1, BLK), block(BLK, BLK + 1))
    last = jnp.where(row <= col, block(2 * BLK, 2 * BLK), spare)
    split_block = block(0, 2 * BLK)
    return jnp.where(
        half == 0,
        jnp.concatenate([first, block(0, BLK), split_block[: BLK // 2]], axis=0),
        jnp.concatenate([split_block[BLK // 2 :], block(BLK, 2 * BLK), last], axis=0),
    )


def unpack(packed):
    row, col = indices()
    first, b01, b02, b12, last = [packed[i * BLK : (i + 1) * BLK] for i in range(5)]
    first_t, last_t = first.T, last.T
    b00 = jnp.where(row <= col, first, first_t)
    b22 = jnp.where(row <= col, last, last_t)
    diagonal = jnp.where(row == 0, jnp.roll(last, 1, 0), jnp.roll(last, 1, 1))
    b11 = jnp.where(row == col, diagonal, jnp.where(row > col, first, first_t))
    trace = jnp.where(row == col, b00 + b11 + b22, 0.0)
    gram = jnp.concatenate(
        [
            jnp.concatenate([b00, b01, b02], axis=1),
            jnp.concatenate([b01.T, b11, b12], axis=1),
            jnp.concatenate([b02.T, b12.T, b22], axis=1),
        ],
        axis=0,
    )
    return gram, jnp.sum(jnp.sum(trace, axis=1, keepdims=True), axis=0, keepdims=True)


def orthogonal_rows(packed, rows):
    gram, total = unpack(packed)
    norm = jnp.sqrt(total) + NORM_EPS
    gram = gram / (norm * norm)
    iterate = (rows.astype(f32) / norm).astype(bf16)
    for iteration in range(ITERS):
        iterate = lax.optimization_barrier(iterate)
        near, high, low = split(gram)
        poly = (B_COEF * near + C_COEF * dot(high, high)).astype(bf16)
        iterate = (A_COEF * iterate.astype(f32) + dot(iterate, poly)).astype(bf16)
        if iteration < ITERS - 1:
            wide = jnp.concatenate([poly, poly], axis=1)
            half = A_COEF * gram + dot(wide, jnp.concatenate([high, low], axis=0))
            _, high, low = split(half)
            tall = jnp.concatenate([poly, poly], axis=0)
            gram = A_COEF * half + dot(jnp.concatenate([high, low], axis=1), tall)
    return iterate


def body(momentum, gradient, weight):
    rows = momentum.shape[1]
    members = 8
    pair = lax.axis_index("pair")
    side = lax.axis_index("side")
    first = 2 * lax.axis_index("replica")

    def rounded(index):
        m = lax.dynamic_slice_in_dim(momentum, index, 2, 0)
        g = lax.dynamic_slice_in_dim(gradient, index, 2, 0)
        return (MOMENTUM_COEF * m + g.astype(f32)).astype(bf16)

    sent = jnp.concatenate([rounded(first), rounded(lax.optimization_barrier(first))], axis=0)
    new_momentum = MOMENTUM_COEF * momentum + gradient.astype(f32)
    owned = lax.all_to_all(sent, ("pair", "side"), split_axis=0, concat_axis=0, tiled=True)
    partial = packed_half(owned.reshape(4 * rows, C), pair)
    own = lax.dynamic_index_in_dim(owned, 2 * pair + side, 0, keepdims=False)
    got = lax.dynamic_index_in_dim(owned, 2 * pair + 1 - side, 0, keepdims=False)
    mine = jnp.concatenate([own, got], axis=0)
    pieces = partial.reshape(members, partial.shape[0] // members, BLK)
    pieces = lax.all_to_all(pieces, "y", split_axis=0, concat_axis=0, tiled=True)
    total = jnp.broadcast_to(jnp.sum(pieces, axis=0)[None], (2 * members,) + pieces.shape[1:])
    packed = lax.all_to_all(total, ("pair", "y"), split_axis=0, concat_axis=0, tiled=True)
    final = orthogonal_rows(packed.reshape(2 * partial.shape[0], BLK), mine)
    own, got = final[:rows], final[rows:]
    got = lax.ppermute(got, "side", [(0, 1), (1, 0)])
    both = jnp.where(side == 0, jnp.stack([own, got]), jnp.stack([got, own]))
    finished = lax.all_gather(both, "replica", axis=0, tiled=True)
    scale = 0.2 * math.sqrt(max(D, C))
    update = (scale * finished.astype(f32) + WEIGHT_DECAY * weight.astype(f32)).astype(bf16)
    return (new_momentum, update)


def solution(mesh):
    devices = mesh.devices.reshape(8, 2, 2, 8, 2)
    grid = Mesh(devices, ("y", "pair", "side", "expert", "replica"))
    placed = P("expert", ("y", "pair", "side"), None)
    return jax.shard_map(
        body,
        mesh=grid,
        in_specs=(placed, placed, placed),
        out_specs=(placed, placed),
        check_vma=False,
    )
```

```python
import math

import jax
import jax.numpy as jnp
from jax import lax
from jax.experimental import pallas as pl
from jax.experimental.pallas import tpu as pltpu
from jax.sharding import Mesh
from jax.sharding import PartitionSpec as P

D = 3584
C = 384
ITERS = 5
BLK = 128

MOMENTUM_COEF = 0.95
NORM_EPS = 1e-07
A_COEF = 3.4445
B_COEF = -4.775
C_COEF = 2.0315
WEIGHT_DECAY = 0.1

f32 = jnp.float32
bf16 = jnp.bfloat16


def dot(a, b):
    return jnp.dot(a, b, preferred_element_type=f32)


def split(value):
    high = value.astype(bf16)
    low = (value - high.astype(f32)).astype(bf16)
    return high, low


def indices():
    row = lax.broadcasted_iota(jnp.int32, (BLK, BLK), 0)
    col = lax.broadcasted_iota(jnp.int32, (BLK, BLK), 1)
    return row, col


def packed_half(rows, half):
    gram = lax.dot_general(rows, rows, (((0,), (0,)), ((), ())), preferred_element_type=f32)
    row, col = indices()

    def block(i, j):
        return lax.slice(gram, (i, j), (i + BLK, j + BLK))

    first = jnp.where(row <= col, block(0, 0), block(BLK, BLK))
    corner = (row == BLK - 1) & (col == 0)
    spare = jnp.where(corner, block(1, BLK), block(BLK, BLK + 1))
    last = jnp.where(row <= col, block(2 * BLK, 2 * BLK), spare)
    split_block = block(0, 2 * BLK)
    return jnp.where(
        half == 0,
        jnp.concatenate([first, block(0, BLK), split_block[: BLK // 2]], axis=0),
        jnp.concatenate([split_block[BLK // 2 :], block(BLK, 2 * BLK), last], axis=0),
    )


def unpack(ref):
    row, col = indices()
    first, b01, b02, b12, last = [ref[i * BLK : (i + 1) * BLK] for i in range(5)]
    first_t, last_t = first.T, last.T
    b00 = jnp.where(row <= col, first, first_t)
    b22 = jnp.where(row <= col, last, last_t)
    corner = jnp.broadcast_to(last[BLK - 1 :, :1], (BLK, BLK))
    diagonal = jnp.where(row == 0, corner, pltpu.roll(last, 1, 1))
    b11 = jnp.where(row == col, diagonal, jnp.where(row > col, first, first_t))
    trace = jnp.where(row == col, b00 + b11 + b22, 0.0)
    gram = jnp.concatenate(
        [
            jnp.concatenate([b00, b01, b02], axis=1),
            jnp.concatenate([b01.T, b11, b12], axis=1),
            jnp.concatenate([b02.T, b12.T, b22], axis=1),
        ],
        axis=0,
    )
    return gram, jnp.sum(jnp.sum(trace, axis=1, keepdims=True), axis=0, keepdims=True)


def advance(iterate, poly):
    return (A_COEF * iterate.astype(f32) + dot(iterate, poly)).astype(bf16)


def chain_kernel(packed_ref, own_ref, got_ref, own_out_ref, got_out_ref, *refs):
    poly_refs, (gram_ref,) = refs[:ITERS], refs[ITERS:]
    gram, total = unpack(packed_ref)
    norm = jnp.sqrt(total) + NORM_EPS
    gram_ref[...] = gram / (norm * norm)
    own_out_ref[...] = (own_ref[...].astype(f32) / norm).astype(bf16)
    iterate = (got_ref[...].astype(f32) / norm).astype(bf16)
    for iteration, poly_ref in enumerate(poly_refs):
        gram = gram_ref[...]
        high, low = split(gram)
        poly = (B_COEF * high.astype(f32) + C_COEF * dot(high, high)).astype(bf16)
        poly_ref[...] = poly
        iterate = advance(iterate, poly)
        if iteration < ITERS - 1:
            wide = jnp.concatenate([poly, poly], axis=1)
            half = A_COEF * gram + dot(wide, jnp.concatenate([high, low], axis=0))
            tall = jnp.concatenate([poly, poly], axis=0)
            gram_ref[...] = A_COEF * half + dot(jnp.concatenate(split(half), axis=1), tall)
    got_out_ref[...] = iterate


def body(momentum, gradient, weight):
    rows = momentum.shape[1]
    members = 8
    pair = lax.axis_index("pair")
    side = lax.axis_index("side")
    first = 2 * lax.axis_index("replica")

    m = lax.dynamic_slice_in_dim(momentum, first, 2, 0)
    g = lax.dynamic_slice_in_dim(gradient, first, 2, 0)
    rounded = (MOMENTUM_COEF * m + g.astype(f32)).astype(bf16)
    sent = jnp.broadcast_to(rounded[None], (2, 2, rows, C)).reshape(4, rows, C)
    owned = lax.all_to_all(sent, ("pair", "side"), split_axis=0, concat_axis=0, tiled=True)
    partial = packed_half(owned.reshape(4 * rows, C), pair)
    own = lax.dynamic_index_in_dim(owned, 2 * pair + side, 0, keepdims=False)
    got = lax.dynamic_index_in_dim(owned, 2 * pair + 1 - side, 0, keepdims=False)
    pieces = partial.reshape(members, partial.shape[0] // members, BLK)
    pieces = lax.all_to_all(pieces, "y", split_axis=0, concat_axis=0, tiled=True)
    late = lax.optimization_barrier((momentum, gradient, pieces))
    new_momentum = MOMENTUM_COEF * late[0] + late[1].astype(f32)
    total = jnp.broadcast_to(jnp.sum(pieces, axis=0)[None], (2 * members,) + pieces.shape[1:])
    packed = lax.all_to_all(total, ("pair", "y"), split_axis=0, concat_axis=0, tiled=True)
    packed, new_momentum = lax.optimization_barrier((packed, new_momentum))
    piece = jax.ShapeDtypeStruct((rows, C), bf16)
    square = jax.ShapeDtypeStruct((C, C), bf16)
    own, got, *polys = pl.pallas_call(
        chain_kernel,
        out_shape=(piece, piece) + (square,) * ITERS,
        scratch_shapes=[pltpu.VMEM((C, C), f32)],
    )(packed.reshape(2 * partial.shape[0], BLK), own, got)
    got = lax.ppermute(got, "side", [(0, 1), (1, 0)])
    for poly in polys:
        own = lax.optimization_barrier(advance(own, poly))
    both = jnp.where(side == 0, jnp.stack([own, got]), jnp.stack([got, own]))
    finished = lax.all_gather(both, "replica", axis=0, tiled=True)
    scale = 0.2 * math.sqrt(max(D, C))
    update = (scale * finished.astype(f32) + WEIGHT_DECAY * weight.astype(f32)).astype(bf16)
    return (new_momentum, update)


def solution(mesh):
    devices = mesh.devices.reshape(8, 2, 2, 8, 2)
    grid = Mesh(devices, ("y", "pair", "side", "expert", "replica"))
    placed = P("expert", ("y", "pair", "side"), None)
    return jax.shard_map(
        body,
        mesh=grid,
        in_specs=(placed, placed, placed),
        out_specs=(placed, placed),
        check_vma=False,
    )
```

```python
import math

import jax
import jax.numpy as jnp
from jax import lax
from jax.experimental import pallas as pl
from jax.experimental.pallas import tpu as pltpu
from jax.sharding import Mesh
from jax.sharding import PartitionSpec as P

D = 3584
C = 384
ITERS = 5
BLK = 128

MOMENTUM_COEF = 0.95
NORM_EPS = 1e-07
A_COEF = 3.4445
B_COEF = -4.775
C_COEF = 2.0315
WEIGHT_DECAY = 0.1

f32 = jnp.float32
bf16 = jnp.bfloat16


def dot(a, b):
    return jnp.dot(a, b, preferred_element_type=f32)


def split(value):
    high = value.astype(bf16)
    low = (value - high.astype(f32)).astype(bf16)
    return high, low


def indices():
    row = lax.broadcasted_iota(jnp.int32, (BLK, BLK), 0)
    col = lax.broadcasted_iota(jnp.int32, (BLK, BLK), 1)
    return row, col


def packed_half(rows, half):
    gram = lax.dot_general(rows, rows, (((0,), (0,)), ((), ())), preferred_element_type=f32)
    row, col = indices()

    def block(i, j):
        return lax.slice(gram, (i, j), (i + BLK, j + BLK))

    first = jnp.where(row <= col, block(0, 0), block(BLK, BLK))
    corner = (row == BLK - 1) & (col == 0)
    spare = jnp.where(corner, block(1, BLK), block(BLK, BLK + 1))
    last = jnp.where(row <= col, block(2 * BLK, 2 * BLK), spare)
    split_block = block(0, 2 * BLK)
    return jnp.where(
        half == 0,
        jnp.concatenate([first, block(0, BLK), split_block[: BLK // 2]], axis=0),
        jnp.concatenate([split_block[BLK // 2 :], block(BLK, 2 * BLK), last], axis=0),
    )


def unpack(ref):
    row, col = indices()
    first, b01, b02, b12, last = [ref[i * BLK : (i + 1) * BLK] for i in range(5)]
    first_t, last_t = first.T, last.T
    b00 = jnp.where(row <= col, first, first_t)
    b22 = jnp.where(row <= col, last, last_t)
    corner = jnp.broadcast_to(last[BLK - 1 :, :1], (BLK, BLK))
    diagonal = jnp.where(row == 0, corner, pltpu.roll(last, 1, 1))
    b11 = jnp.where(row == col, diagonal, jnp.where(row > col, first, first_t))
    trace = jnp.where(row == col, b00 + b11 + b22, 0.0)
    gram = jnp.concatenate(
        [
            jnp.concatenate([b00, b01, b02], axis=1),
            jnp.concatenate([b01.T, b11, b12], axis=1),
            jnp.concatenate([b02.T, b12.T, b22], axis=1),
        ],
        axis=0,
    )
    return gram, jnp.sum(jnp.sum(trace, axis=1, keepdims=True), axis=0, keepdims=True)


def chain_kernel(packed_ref, rows_ref, out_ref, gram_ref, x_ref):
    gram, total = unpack(packed_ref)
    norm = jnp.sqrt(total) + NORM_EPS
    gram_ref[...] = gram / (norm * norm)
    x_ref[...] = (rows_ref[...].astype(f32) / norm).astype(bf16)

    def polynomial():
        g = gram_ref[...].astype(bf16)
        return (B_COEF * g.astype(f32) + C_COEF * dot(g, g)).astype(bf16)

    def advance(poly):
        iterate = x_ref[...]
        return (A_COEF * iterate.astype(f32) + dot(iterate, poly)).astype(bf16)

    def step(iteration, carry):
        poly = polynomial()
        gram = gram_ref[...]
        high, low = split(gram)
        wide = jnp.concatenate([poly, poly], axis=1)
        half = A_COEF * gram + dot(wide, jnp.concatenate([high, low], axis=0))
        high, low = split(half)
        tall = jnp.concatenate([poly, poly], axis=0)
        gram_ref[...] = A_COEF * half + dot(jnp.concatenate([high, low], axis=1), tall)
        x_ref[...] = advance(poly)
        return carry

    lax.fori_loop(0, ITERS - 1, step, 0)
    out_ref[...] = advance(polynomial())


def body(momentum, gradient, weight):
    mats, rows, _ = momentum.shape
    members = 8
    sent = (MOMENTUM_COEF * momentum + gradient.astype(f32)).astype(bf16)
    owned = lax.all_to_all(sent, "x", split_axis=0, concat_axis=0, tiled=True)
    late_momentum, late_gradient, _ = lax.optimization_barrier((momentum, gradient, sent))
    new_momentum = MOMENTUM_COEF * late_momentum + late_gradient.astype(f32)
    owned, new_momentum = lax.optimization_barrier((owned, new_momentum))
    owned = owned.reshape(mats * rows, C)
    partial = packed_half(owned, lax.axis_index("replica"))
    pieces = partial.reshape(members, partial.shape[0] // members, BLK)
    pieces = lax.all_to_all(pieces, "y", split_axis=0, concat_axis=0, tiled=True)
    total = jnp.broadcast_to(jnp.sum(pieces, axis=0)[None], pieces.shape)
    half = lax.all_to_all(total, "y", split_axis=0, concat_axis=0, tiled=True)
    packed = lax.all_gather(half.reshape(partial.shape), "replica", axis=0, tiled=True)
    final = pl.pallas_call(
        chain_kernel,
        out_shape=jax.ShapeDtypeStruct(owned.shape, bf16),
        scratch_shapes=[pltpu.VMEM((C, C), f32), pltpu.VMEM(owned.shape, bf16)],
    )(packed, owned)
    final = final.reshape(mats, rows, C)
    finished = lax.all_to_all(final, "x", split_axis=0, concat_axis=0, tiled=True)
    scale = 0.2 * math.sqrt(max(D, C))
    update = (scale * finished.astype(f32) + WEIGHT_DECAY * weight.astype(f32)).astype(bf16)
    return (new_momentum, update)


def solution(mesh):
    devices = mesh.devices.reshape(8, 4, 8, 2)
    grid = Mesh(devices, ("y", "x", "expert", "replica"))
    placed = P("expert", ("y", "x"), None)
    return jax.shard_map(
        body,
        mesh=grid,
        in_specs=(placed, placed, placed),
        out_specs=(placed, placed),
        check_vma=False,
    )
```

```python
import math

import jax
import jax.numpy as jnp
from jax import lax
from jax.experimental import pallas as pl
from jax.experimental.pallas import tpu as pltpu
from jax.sharding import Mesh
from jax.sharding import PartitionSpec as P

D = 3584
C = 384
ITERS = 5
BLK = 128

MOMENTUM_COEF = 0.95
NORM_EPS = 1e-07
A_COEF = 3.4445
B_COEF = -4.775
C_COEF = 2.0315
WEIGHT_DECAY = 0.1

f32 = jnp.float32
bf16 = jnp.bfloat16


def dot(a, b):
    return jnp.dot(a, b, preferred_element_type=f32)


def split(value):
    high = value.astype(bf16)
    low = (value - high.astype(f32)).astype(bf16)
    return high, low


def indices():
    row = lax.broadcasted_iota(jnp.int32, (BLK, BLK), 0)
    col = lax.broadcasted_iota(jnp.int32, (BLK, BLK), 1)
    return row, col


def packed_half(rows, half):
    gram = lax.dot_general(rows, rows, (((0,), (0,)), ((), ())), preferred_element_type=f32)
    row, col = indices()

    def block(i, j):
        return lax.slice(gram, (i, j), (i + BLK, j + BLK))

    first = jnp.where(row <= col, block(0, 0), block(BLK, BLK))
    corner = (row == BLK - 1) & (col == 0)
    spare = jnp.where(corner, block(1, BLK), block(BLK, BLK + 1))
    last = jnp.where(row <= col, block(2 * BLK, 2 * BLK), spare)
    split_block = block(0, 2 * BLK)
    return jnp.where(
        half == 0,
        jnp.concatenate([first, block(0, BLK), split_block[: BLK // 2]], axis=0),
        jnp.concatenate([split_block[BLK // 2 :], block(BLK, 2 * BLK), last], axis=0),
    )


def unpack(ref):
    row, col = indices()
    first, b01, b02, b12, last = [ref[i * BLK : (i + 1) * BLK] for i in range(5)]
    first_t, last_t = first.T, last.T
    b00 = jnp.where(row <= col, first, first_t)
    b22 = jnp.where(row <= col, last, last_t)
    corner = jnp.broadcast_to(last[BLK - 1 :, :1], (BLK, BLK))
    diagonal = jnp.where(row == 0, corner, pltpu.roll(last, 1, 1))
    b11 = jnp.where(row == col, diagonal, jnp.where(row > col, first, first_t))
    trace = jnp.where(row == col, b00 + b11 + b22, 0.0)
    gram = jnp.concatenate(
        [
            jnp.concatenate([b00, b01, b02], axis=1),
            jnp.concatenate([b01.T, b11, b12], axis=1),
            jnp.concatenate([b02.T, b12.T, b22], axis=1),
        ],
        axis=0,
    )
    return gram, jnp.sum(jnp.sum(trace, axis=1, keepdims=True), axis=0, keepdims=True)


def chain_kernel(
    source_ref, own_ref, got_ref, own_out_ref, got_out_ref, packed_ref, gram_ref, x_ref, sems
):
    count = own_ref.shape[0]
    copies = [
        pltpu.make_async_copy(
            source_ref.at[pl.ds(i * BLK, BLK)], packed_ref.at[pl.ds(i * BLK, BLK)], sems.at[i]
        )
        for i in range(5)
    ]
    for copy in copies:
        copy.start()
    for copy in copies:
        copy.wait()
    gram, total = unpack(packed_ref)
    norm = jnp.sqrt(total) + NORM_EPS
    gram_ref[...] = gram / (norm * norm)
    x_ref[:count] = (own_ref[...].astype(f32) / norm).astype(bf16)
    x_ref[count:] = (got_ref[...].astype(f32) / norm).astype(bf16)

    def polynomial():
        g = gram_ref[...].astype(bf16)
        return (B_COEF * g.astype(f32) + C_COEF * dot(g, g)).astype(bf16)

    def advance(poly):
        iterate = x_ref[...]
        return (A_COEF * iterate.astype(f32) + dot(iterate, poly)).astype(bf16)

    def step(iteration, carry):
        poly = polynomial()
        gram = gram_ref[...]
        high, low = split(gram)
        wide = jnp.concatenate([poly, poly], axis=1)
        half = A_COEF * gram + dot(wide, jnp.concatenate([high, low], axis=0))
        high, low = split(half)
        tall = jnp.concatenate([poly, poly], axis=0)
        gram_ref[...] = A_COEF * half + dot(jnp.concatenate([high, low], axis=1), tall)
        x_ref[...] = advance(poly)
        return carry

    lax.fori_loop(0, ITERS - 1, step, 0)
    iterate = advance(polynomial())
    own_out_ref[...] = iterate[:count]
    got_out_ref[...] = iterate[count:]


def body(momentum, gradient, weight):
    rows = momentum.shape[1]
    members = 8
    pair = lax.axis_index("pair")
    side = lax.axis_index("side")
    first = 2 * lax.axis_index("replica")

    m = lax.dynamic_slice_in_dim(momentum, first, 2, 0)
    g = lax.dynamic_slice_in_dim(gradient, first, 2, 0)
    rounded = (MOMENTUM_COEF * m + g.astype(f32)).astype(bf16)
    sent = jnp.broadcast_to(rounded[None], (2, 2, rows, C)).reshape(4, rows, C)
    owned = lax.all_to_all(sent, ("pair", "side"), split_axis=0, concat_axis=0, tiled=True)
    partial = packed_half(owned.reshape(4 * rows, C), pair)
    own = lax.dynamic_index_in_dim(owned, 2 * pair + side, 0, keepdims=False)
    got = lax.dynamic_index_in_dim(owned, 2 * pair + 1 - side, 0, keepdims=False)
    pieces = partial.reshape(members, partial.shape[0] // members, BLK)
    pieces = lax.all_to_all(pieces, "y", split_axis=0, concat_axis=0, tiled=True)
    late_momentum, late_gradient, _ = lax.optimization_barrier((momentum, gradient, pieces))
    new_momentum = MOMENTUM_COEF * late_momentum + late_gradient.astype(f32)
    total = jnp.broadcast_to(jnp.sum(pieces, axis=0)[None], (2 * members,) + pieces.shape[1:])
    packed = lax.all_to_all(total, ("pair", "y"), split_axis=0, concat_axis=0, tiled=True)
    packed, new_momentum = lax.optimization_barrier((packed, new_momentum))
    piece = jax.ShapeDtypeStruct((rows, C), bf16)
    own, got = pl.pallas_call(
        chain_kernel,
        out_shape=(piece, piece),
        in_specs=[
            pl.BlockSpec(memory_space=pl.ANY),
            pl.BlockSpec(memory_space=pltpu.VMEM),
            pl.BlockSpec(memory_space=pltpu.VMEM),
        ],
        scratch_shapes=[
            pltpu.VMEM((5 * BLK, BLK), f32),
            pltpu.VMEM((C, C), f32),
            pltpu.VMEM((2 * rows, C), bf16),
            pltpu.SemaphoreType.DMA((5,)),
        ],
    )(
        packed.reshape(2 * partial.shape[0], BLK), own, got
    )
    got = lax.ppermute(got, "side", [(0, 1), (1, 0)])
    both = jnp.where(side == 0, jnp.stack([own, got]), jnp.stack([got, own]))
    finished = lax.all_gather(both, "replica", axis=0, tiled=True)
    scale = 0.2 * math.sqrt(max(D, C))
    update = (scale * finished.astype(f32) + WEIGHT_DECAY * weight.astype(f32)).astype(bf16)
    return (new_momentum, update)


def solution(mesh):
    devices = mesh.devices.reshape(8, 2, 2, 8, 2)
    grid = Mesh(devices, ("y", "pair", "side", "expert", "replica"))
    placed = P("expert", ("y", "pair", "side"), None)
    return jax.shard_map(
        body,
        mesh=grid,
        in_specs=(placed, placed, placed),
        out_specs=(placed, placed),
        check_vma=False,
    )
```

```python
import math

import jax
import jax.numpy as jnp
from jax import lax
from jax.experimental import pallas as pl
from jax.experimental.pallas import tpu as pltpu
from jax.sharding import Mesh
from jax.sharding import PartitionSpec as P

D = 3584
C = 384
ITERS = 5
BLK = 128

MOMENTUM_COEF = 0.95
NORM_EPS = 1e-07
A_COEF = 3.4445
B_COEF = -4.775
C_COEF = 2.0315
WEIGHT_DECAY = 0.1

f32 = jnp.float32
bf16 = jnp.bfloat16


def dot(a, b):
    return jnp.dot(a, b, preferred_element_type=f32)


def split(value):
    high = value.astype(bf16)
    low = (value - high.astype(f32)).astype(bf16)
    return high, low


def indices():
    row = lax.broadcasted_iota(jnp.int32, (BLK, BLK), 0)
    col = lax.broadcasted_iota(jnp.int32, (BLK, BLK), 1)
    return row, col


def packed_half(rows, half):
    gram = lax.dot_general(rows, rows, (((0,), (0,)), ((), ())), preferred_element_type=f32)
    row, col = indices()

    def block(i, j):
        return lax.slice(gram, (i, j), (i + BLK, j + BLK))

    first = jnp.where(row <= col, block(0, 0), block(BLK, BLK))
    corner = (row == BLK - 1) & (col == 0)
    spare = jnp.where(corner, block(1, BLK), block(BLK, BLK + 1))
    last = jnp.where(row <= col, block(2 * BLK, 2 * BLK), spare)
    split_block = block(0, 2 * BLK)
    return jnp.where(
        half == 0,
        jnp.concatenate([first, block(0, BLK), split_block[: BLK // 2]], axis=0),
        jnp.concatenate([split_block[BLK // 2 :], block(BLK, 2 * BLK), last], axis=0),
    )


def unpack(ref):
    row, col = indices()
    first, b01, b02, b12, last = [ref[i * BLK : (i + 1) * BLK] for i in range(5)]
    first_t, last_t = first.T, last.T
    b00 = jnp.where(row <= col, first, first_t)
    b22 = jnp.where(row <= col, last, last_t)
    corner = jnp.broadcast_to(last[BLK - 1 :, :1], (BLK, BLK))
    diagonal = jnp.where(row == 0, corner, pltpu.roll(last, 1, 1))
    b11 = jnp.where(row == col, diagonal, jnp.where(row > col, first, first_t))
    trace = jnp.where(row == col, b00 + b11 + b22, 0.0)
    gram = jnp.concatenate(
        [
            jnp.concatenate([b00, b01, b02], axis=1),
            jnp.concatenate([b01.T, b11, b12], axis=1),
            jnp.concatenate([b02.T, b12.T, b22], axis=1),
        ],
        axis=0,
    )
    return gram, jnp.sum(jnp.sum(trace, axis=1, keepdims=True), axis=0, keepdims=True)


def chain_kernel(packed_ref, own_ref, got_ref, own_out_ref, got_out_ref, gram_ref, x_ref):
    count = own_ref.shape[0]
    gram, total = unpack(packed_ref)
    norm = jnp.sqrt(total) + NORM_EPS
    gram_ref[...] = gram / (norm * norm)
    x_ref[:count] = (own_ref[...].astype(f32) / norm).astype(bf16)
    x_ref[count:] = (got_ref[...].astype(f32) / norm).astype(bf16)

    def polynomial():
        g = gram_ref[...].astype(bf16)
        return (B_COEF * g.astype(f32) + C_COEF * dot(g, g)).astype(bf16)

    def advance(poly):
        iterate = x_ref[...]
        return (A_COEF * iterate.astype(f32) + dot(iterate, poly)).astype(bf16)

    def step(iteration, carry):
        poly = polynomial()
        gram = gram_ref[...]
        high, low = split(gram)
        wide = jnp.concatenate([poly, poly], axis=1)
        half = A_COEF * gram + dot(wide, jnp.concatenate([high, low], axis=0))
        high, low = split(half)
        tall = jnp.concatenate([poly, poly], axis=0)
        gram_ref[...] = A_COEF * half + dot(jnp.concatenate([high, low], axis=1), tall)
        x_ref[...] = advance(poly)
        return carry

    lax.fori_loop(0, ITERS - 1, step, 0)
    iterate = advance(polynomial())
    own_out_ref[...] = iterate[:count]
    got_out_ref[...] = iterate[count:]


def body(momentum, gradient, weight):
    rows = momentum.shape[1]
    members = 8
    pair = lax.axis_index("pair")
    side = lax.axis_index("side")
    first = 2 * lax.axis_index("replica")

    m = lax.dynamic_slice_in_dim(momentum, first, 2, 0)
    g = lax.dynamic_slice_in_dim(gradient, first, 2, 0)
    rounded = (MOMENTUM_COEF * m + g.astype(f32)).astype(bf16)
    sent = jnp.broadcast_to(rounded[None], (2, 2, rows, C)).reshape(4, rows, C)
    owned = lax.all_to_all(sent, ("pair", "side"), split_axis=0, concat_axis=0, tiled=True)
    partial = packed_half(owned.reshape(4 * rows, C), pair)
    own = lax.dynamic_index_in_dim(owned, 2 * pair + side, 0, keepdims=False)
    got = lax.dynamic_index_in_dim(owned, 2 * pair + 1 - side, 0, keepdims=False)
    pieces = partial.reshape(members, partial.shape[0] // members, BLK)
    pieces = lax.all_to_all(pieces, "y", split_axis=0, concat_axis=0, tiled=True)
    late_momentum, late_gradient, _ = lax.optimization_barrier((momentum, gradient, pieces))
    new_momentum = MOMENTUM_COEF * late_momentum + late_gradient.astype(f32)
    total = jnp.broadcast_to(jnp.sum(pieces, axis=0)[None], (2 * members,) + pieces.shape[1:])
    packed = lax.all_to_all(total, ("pair", "y"), split_axis=0, concat_axis=0, tiled=True)
    packed, new_momentum = lax.optimization_barrier((packed, new_momentum))
    piece = jax.ShapeDtypeStruct((rows, C), bf16)
    own, got = pl.pallas_call(
        chain_kernel,
        out_shape=(piece, piece),
        scratch_shapes=[pltpu.VMEM((C, C), f32), pltpu.VMEM((2 * rows, C), bf16)],
    )(
        packed.reshape(2 * partial.shape[0], BLK), own, got
    )
    got = lax.ppermute(got, "side", [(0, 1), (1, 0)])
    both = jnp.where(side == 0, jnp.stack([own, got]), jnp.stack([got, own]))
    scale = 0.2 * math.sqrt(max(D, C))
    w = lax.dynamic_slice_in_dim(weight, first, 2, 0)
    update = (scale * both.astype(f32) + WEIGHT_DECAY * w.astype(f32)).astype(bf16)
    return (new_momentum, lax.all_gather(update, "replica", axis=0, tiled=True))


def solution(mesh):
    devices = mesh.devices.reshape(8, 2, 2, 8, 2)
    grid = Mesh(devices, ("y", "pair", "side", "expert", "replica"))
    placed = P("expert", ("y", "pair", "side"), None)
    return jax.shard_map(
        body,
        mesh=grid,
        in_specs=(placed, placed, placed),
        out_specs=(placed, placed),
        check_vma=False,
    )
```

```python
import math

import jax
import jax.numpy as jnp
from jax import lax
from jax.experimental import pallas as pl
from jax.experimental.pallas import tpu as pltpu
from jax.sharding import Mesh
from jax.sharding import PartitionSpec as P

D = 3584
C = 384
ITERS = 5
BLK = 128

MOMENTUM_COEF = 0.95
NORM_EPS = 1e-07
A_COEF = 3.4445
B_COEF = -4.775
C_COEF = 2.0315
WEIGHT_DECAY = 0.1

f32 = jnp.float32
bf16 = jnp.bfloat16


def dot(a, b):
    return jnp.dot(a, b, preferred_element_type=f32)


def split(value):
    high = value.astype(bf16)
    low = (value - high.astype(f32)).astype(bf16)
    return high, low


def indices():
    row = lax.broadcasted_iota(jnp.int32, (BLK, BLK), 0)
    col = lax.broadcasted_iota(jnp.int32, (BLK, BLK), 1)
    return row, col


def packed_half(rows, half):
    gram = lax.dot_general(rows, rows, (((0,), (0,)), ((), ())), preferred_element_type=f32)
    row, col = indices()

    def block(i, j):
        return lax.slice(gram, (i, j), (i + BLK, j + BLK))

    first = jnp.where(row <= col, block(0, 0), block(BLK, BLK))
    corner = (row == BLK - 1) & (col == 0)
    spare = jnp.where(corner, block(1, BLK), block(BLK, BLK + 1))
    last = jnp.where(row <= col, block(2 * BLK, 2 * BLK), spare)
    split_block = block(0, 2 * BLK)
    return jnp.where(
        half == 0,
        jnp.concatenate([first, block(0, BLK), split_block[: BLK // 2]], axis=0),
        jnp.concatenate([split_block[BLK // 2 :], block(BLK, 2 * BLK), last], axis=0),
    )


def unpack(ref):
    row, col = indices()
    first, b01, b02, b12, last = [ref[i * BLK : (i + 1) * BLK] for i in range(5)]
    first_t, last_t = first.T, last.T
    b00 = jnp.where(row <= col, first, first_t)
    b22 = jnp.where(row <= col, last, last_t)
    corner = jnp.broadcast_to(last[BLK - 1 :, :1], (BLK, BLK))
    diagonal = jnp.where(row == 0, corner, pltpu.roll(last, 1, 1))
    b11 = jnp.where(row == col, diagonal, jnp.where(row > col, first, first_t))
    trace = jnp.where(row == col, b00 + b11 + b22, 0.0)
    gram = jnp.concatenate(
        [
            jnp.concatenate([b00, b01, b02], axis=1),
            jnp.concatenate([b01.T, b11, b12], axis=1),
            jnp.concatenate([b02.T, b12.T, b22], axis=1),
        ],
        axis=0,
    )
    return gram, jnp.sum(jnp.sum(trace, axis=1, keepdims=True), axis=0, keepdims=True)


def chain_kernel(packed_ref, own_ref, got_ref, own_out_ref, got_out_ref, gram_ref, x_ref):
    count = own_ref.shape[0]
    gram, total = unpack(packed_ref)
    norm = jnp.sqrt(total) + NORM_EPS
    gram_ref[...] = gram * (1.0 / (norm * norm))
    x_ref[:count] = (own_ref[...].astype(f32) / norm).astype(bf16)
    x_ref[count:] = (got_ref[...].astype(f32) / norm).astype(bf16)

    def polynomial():
        g = gram_ref[...].astype(bf16)
        return (B_COEF * g.astype(f32) + C_COEF * dot(g, g)).astype(bf16)

    def advance(poly):
        iterate = x_ref[...]
        return (A_COEF * iterate.astype(f32) + dot(iterate, poly)).astype(bf16)

    def step(iteration, carry):
        poly = polynomial()
        gram = gram_ref[...]
        high, low = split(gram)
        wide = jnp.concatenate([poly, poly], axis=1)
        half = A_COEF * gram + dot(wide, jnp.concatenate([high, low], axis=0))
        high, low = split(half)
        tall = jnp.concatenate([poly, poly], axis=0)
        gram_ref[...] = A_COEF * half + dot(jnp.concatenate([high, low], axis=1), tall)
        x_ref[...] = advance(poly)
        return carry

    lax.fori_loop(0, ITERS - 1, step, 0)
    iterate = advance(polynomial())
    own_out_ref[...] = iterate[:count]
    got_out_ref[...] = iterate[count:]


def body(momentum, gradient, weight):
    rows = momentum.shape[1]
    members = 8
    pair = lax.axis_index("pair")
    side = lax.axis_index("side")
    first = 2 * lax.axis_index("replica")

    m = lax.dynamic_slice_in_dim(momentum, first, 2, 0)
    g = lax.dynamic_slice_in_dim(gradient, first, 2, 0)
    rounded = (MOMENTUM_COEF * m + g.astype(f32)).astype(bf16)
    sent = jnp.broadcast_to(rounded[None], (2, 2, rows, C)).reshape(4, rows, C)
    owned = lax.all_to_all(sent, ("pair", "side"), split_axis=0, concat_axis=0, tiled=True)
    partial = packed_half(owned.reshape(4 * rows, C), pair)
    own = lax.dynamic_index_in_dim(owned, 2 * pair + side, 0, keepdims=False)
    got = lax.dynamic_index_in_dim(owned, 2 * pair + 1 - side, 0, keepdims=False)
    pieces = partial.reshape(members, partial.shape[0] // members, BLK)
    pieces = lax.all_to_all(pieces, "y", split_axis=0, concat_axis=0, tiled=True)
    late_momentum, late_gradient, _ = lax.optimization_barrier((momentum, gradient, pieces))
    new_momentum = MOMENTUM_COEF * late_momentum + late_gradient.astype(f32)
    total = jnp.broadcast_to(jnp.sum(pieces, axis=0)[None], (2 * members,) + pieces.shape[1:])
    packed = lax.all_to_all(total, ("pair", "y"), split_axis=0, concat_axis=0, tiled=True)
    packed, new_momentum = lax.optimization_barrier((packed, new_momentum))
    piece = jax.ShapeDtypeStruct((rows, C), bf16)
    own, got = pl.pallas_call(
        chain_kernel,
        out_shape=(piece, piece),
        scratch_shapes=[pltpu.VMEM((C, C), f32), pltpu.VMEM((2 * rows, C), bf16)],
    )(
        packed.reshape(2 * partial.shape[0], BLK), own, got
    )
    got = lax.ppermute(got, "side", [(0, 1), (1, 0)])
    both = jnp.where(side == 0, jnp.stack([own, got]), jnp.stack([got, own]))
    finished = lax.all_gather(both, "replica", axis=0, tiled=True)
    scale = 0.2 * math.sqrt(max(D, C))
    update = (scale * finished.astype(f32) + WEIGHT_DECAY * weight.astype(f32)).astype(bf16)
    return (new_momentum, update)


def solution(mesh):
    devices = mesh.devices.reshape(8, 2, 2, 8, 2)
    grid = Mesh(devices, ("y", "pair", "side", "expert", "replica"))
    placed = P("expert", ("y", "pair", "side"), None)
    return jax.shard_map(
        body,
        mesh=grid,
        in_specs=(placed, placed, placed),
        out_specs=(placed, placed),
        check_vma=False,
    )
```

```python
import math

import jax
import jax.numpy as jnp
from jax import lax
from jax.experimental import pallas as pl
from jax.experimental.pallas import tpu as pltpu
from jax.sharding import Mesh
from jax.sharding import PartitionSpec as P

D = 3584
C = 384
ITERS = 5
BLK = 128

MOMENTUM_COEF = 0.95
NORM_EPS = 1e-07
A_COEF = 3.4445
B_COEF = -4.775
C_COEF = 2.0315
WEIGHT_DECAY = 0.1

f32 = jnp.float32
bf16 = jnp.bfloat16


def dot(a, b):
    return jnp.dot(a, b, preferred_element_type=f32)


def split(value):
    high = value.astype(bf16)
    low = (value - high.astype(f32)).astype(bf16)
    return high, low


def indices():
    row = lax.broadcasted_iota(jnp.int32, (BLK, BLK), 0)
    col = lax.broadcasted_iota(jnp.int32, (BLK, BLK), 1)
    return row, col


def pack(rows):
    gram = lax.dot_general(rows, rows, (((0,), (0,)), ((), ())), preferred_element_type=f32)
    row, col = indices()

    def block(i, j):
        return lax.slice(gram, (i, j), (i + BLK, j + BLK))

    first = jnp.where(row <= col, block(0, 0), block(BLK, BLK))
    corner = (row == BLK - 1) & (col == 0)
    spare = jnp.where(corner, block(1, BLK), block(BLK, BLK + 1))
    last = jnp.where(row <= col, block(2 * BLK, 2 * BLK), spare)
    return jnp.concatenate(
        [first, block(0, BLK), block(0, 2 * BLK), block(BLK, 2 * BLK), last], axis=0
    )


def unpack(ref):
    row, col = indices()
    first, b01, b02, b12, last = [ref[i * BLK : (i + 1) * BLK] for i in range(5)]
    first_t, last_t = first.T, last.T
    b00 = jnp.where(row <= col, first, first_t)
    b22 = jnp.where(row <= col, last, last_t)
    corner = jnp.broadcast_to(last[BLK - 1 :, :1], (BLK, BLK))
    diagonal = jnp.where(row == 0, corner, pltpu.roll(last, 1, 1))
    b11 = jnp.where(row == col, diagonal, jnp.where(row > col, first, first_t))
    trace = jnp.where(row == col, b00 + b11 + b22, 0.0)
    gram = jnp.concatenate(
        [
            jnp.concatenate([b00, b01, b02], axis=1),
            jnp.concatenate([b01.T, b11, b12], axis=1),
            jnp.concatenate([b02.T, b12.T, b22], axis=1),
        ],
        axis=0,
    )
    return gram, jnp.sum(jnp.sum(trace, axis=1, keepdims=True), axis=0, keepdims=True)


def chain_kernel(packed_ref, own_ref, got_ref, own_out_ref, got_out_ref, gram_ref, x_ref):
    count = own_ref.shape[0]
    gram, total = unpack(packed_ref)
    norm = jnp.sqrt(total) + NORM_EPS
    gram_ref[...] = gram / (norm * norm)
    x_ref[:count] = (own_ref[...].astype(f32) / norm).astype(bf16)
    x_ref[count:] = (got_ref[...].astype(f32) / norm).astype(bf16)

    def polynomial():
        g = gram_ref[...].astype(bf16)
        return (B_COEF * g.astype(f32) + C_COEF * dot(g, g)).astype(bf16)

    def advance(poly):
        iterate = x_ref[...]
        return (A_COEF * iterate.astype(f32) + dot(iterate, poly)).astype(bf16)

    def step(iteration, carry):
        poly = polynomial()
        gram = gram_ref[...]
        high, low = split(gram)
        wide = jnp.concatenate([poly, poly], axis=1)
        half = A_COEF * gram + dot(wide, jnp.concatenate([high, low], axis=0))
        high, low = split(half)
        tall = jnp.concatenate([poly, poly], axis=0)
        gram_ref[...] = A_COEF * half + dot(jnp.concatenate([high, low], axis=1), tall)
        x_ref[...] = advance(poly)
        return carry

    lax.fori_loop(0, ITERS - 1, step, 0)
    iterate = advance(polynomial())
    own_out_ref[...] = iterate[:count]
    got_out_ref[...] = iterate[count:]


def body(momentum, gradient, weight):
    rows = momentum.shape[1]
    members = 16
    side = lax.axis_index("side")
    first = 2 * lax.axis_index("replica")

    def rounded(index):
        m = lax.dynamic_index_in_dim(momentum, index, 0, keepdims=False)
        g = lax.dynamic_index_in_dim(gradient, index, 0, keepdims=False)
        return (MOMENTUM_COEF * m + g.astype(f32)).astype(bf16)

    got = lax.ppermute(rounded(first + 1 - side), "side", [(0, 1), (1, 0)])
    own = rounded(first + side)
    new_momentum = MOMENTUM_COEF * momentum + gradient.astype(f32)
    partial = pack(jnp.concatenate([own, got], axis=0))
    pieces = partial.reshape(members, partial.shape[0] // members, BLK)
    pieces = lax.all_to_all(pieces, ("pair", "y"), split_axis=0, concat_axis=0, tiled=True)
    total = jnp.broadcast_to(jnp.sum(pieces, axis=0)[None], pieces.shape)
    packed = lax.all_to_all(total, ("pair", "y"), split_axis=0, concat_axis=0, tiled=True)
    piece = jax.ShapeDtypeStruct((rows, C), bf16)
    own, got = pl.pallas_call(
        chain_kernel,
        out_shape=(piece, piece),
        scratch_shapes=[pltpu.VMEM((C, C), f32), pltpu.VMEM((2 * rows, C), bf16)],
    )(packed.reshape(partial.shape), own, got)
    got = lax.ppermute(got, "side", [(0, 1), (1, 0)])
    both = jnp.where(side == 0, jnp.stack([own, got]), jnp.stack([got, own]))
    finished = lax.all_gather(both, "replica", axis=0, tiled=True)
    scale = 0.2 * math.sqrt(max(D, C))
    update = (scale * finished.astype(f32) + WEIGHT_DECAY * weight.astype(f32)).astype(bf16)
    return (new_momentum, update)


def solution(mesh):
    devices = mesh.devices.reshape(8, 2, 2, 8, 2)
    grid = Mesh(devices, ("y", "pair", "side", "expert", "replica"))
    placed = P("expert", ("y", "pair", "side"), None)
    return jax.shard_map(
        body,
        mesh=grid,
        in_specs=(placed, placed, placed),
        out_specs=(placed, placed),
        check_vma=False,
    )
```

```python
import math

import jax
import jax.numpy as jnp
from jax import lax
from jax.experimental import pallas as pl
from jax.experimental.pallas import tpu as pltpu
from jax.sharding import Mesh
from jax.sharding import PartitionSpec as P

D = 3584
C = 384
ITERS = 5
BLK = 128

MOMENTUM_COEF = 0.95
NORM_EPS = 1e-07
A_COEF = 3.4445
B_COEF = -4.775
C_COEF = 2.0315
WEIGHT_DECAY = 0.1

f32 = jnp.float32
bf16 = jnp.bfloat16


def dot(a, b):
    return jnp.dot(a, b, preferred_element_type=f32)


def split(value):
    high = value.astype(bf16)
    low = (value - high.astype(f32)).astype(bf16)
    return high, low


def indices():
    row = lax.broadcasted_iota(jnp.int32, (BLK, BLK), 0)
    col = lax.broadcasted_iota(jnp.int32, (BLK, BLK), 1)
    return row, col


def pack(rows):
    gram = lax.dot_general(rows, rows, (((0,), (0,)), ((), ())), preferred_element_type=f32)
    row, col = indices()

    def block(i, j):
        return lax.slice(gram, (i, j), (i + BLK, j + BLK))

    first = jnp.where(row <= col, block(0, 0), block(BLK, BLK))
    corner = (row == BLK - 1) & (col == 0)
    spare = jnp.where(corner, block(1, BLK), block(BLK, BLK + 1))
    last = jnp.where(row <= col, block(2 * BLK, 2 * BLK), spare)
    return jnp.concatenate(
        [first, block(0, BLK), block(0, 2 * BLK), block(BLK, 2 * BLK), last], axis=0
    )


def unpack(ref):
    row, col = indices()
    first, b01, b02, b12, last = [ref[i * BLK : (i + 1) * BLK] for i in range(5)]
    first_t, last_t = first.T, last.T
    b00 = jnp.where(row <= col, first, first_t)
    b22 = jnp.where(row <= col, last, last_t)
    corner = jnp.broadcast_to(last[BLK - 1 :, :1], (BLK, BLK))
    diagonal = jnp.where(row == 0, corner, pltpu.roll(last, 1, 1))
    b11 = jnp.where(row == col, diagonal, jnp.where(row > col, first, first_t))
    trace = jnp.where(row == col, b00 + b11 + b22, 0.0)
    gram = jnp.concatenate(
        [
            jnp.concatenate([b00, b01, b02], axis=1),
            jnp.concatenate([b01.T, b11, b12], axis=1),
            jnp.concatenate([b02.T, b12.T, b22], axis=1),
        ],
        axis=0,
    )
    return gram, jnp.sum(jnp.sum(trace, axis=1, keepdims=True), axis=0, keepdims=True)


def chain_kernel(packed_ref, own_ref, got_ref, own_out_ref, got_out_ref, gram_ref, x_ref):
    count = own_ref.shape[0]
    gram, total = unpack(packed_ref)
    norm = jnp.sqrt(total) + NORM_EPS
    gram_ref[...] = gram / (norm * norm)
    x_ref[:count] = (own_ref[...].astype(f32) / norm).astype(bf16)
    x_ref[count:] = (got_ref[...].astype(f32) / norm).astype(bf16)

    def polynomial():
        g = gram_ref[...].astype(bf16)
        return (B_COEF * g.astype(f32) + C_COEF * dot(g, g)).astype(bf16)

    def advance(poly):
        iterate = x_ref[...]
        return (A_COEF * iterate.astype(f32) + dot(iterate, poly)).astype(bf16)

    def step(iteration, carry):
        poly = polynomial()
        gram = gram_ref[...]
        high, low = split(gram)
        wide = jnp.concatenate([poly, poly], axis=1)
        half = A_COEF * gram + dot(wide, jnp.concatenate([high, low], axis=0))
        high, low = split(half)
        tall = jnp.concatenate([poly, poly], axis=0)
        gram_ref[...] = A_COEF * half + dot(jnp.concatenate([high, low], axis=1), tall)
        x_ref[...] = advance(poly)
        return carry

    lax.fori_loop(0, ITERS - 1, step, 0)
    iterate = advance(polynomial())
    own_out_ref[...] = iterate[:count]
    got_out_ref[...] = iterate[count:]


def body(momentum, gradient, weight):
    rows = momentum.shape[1]
    members = 16
    side = lax.axis_index("side")
    first = 2 * lax.axis_index("replica")

    def rounded(new, old, index):
        m = lax.dynamic_index_in_dim(old, index, 0, keepdims=False)
        g = lax.dynamic_index_in_dim(new, index, 0, keepdims=False)
        return (MOMENTUM_COEF * m + g.astype(f32)).astype(bf16)

    sent = rounded(gradient, momentum, first + 1 - side)
    later = lax.optimization_barrier((gradient, momentum, sent))
    got = lax.ppermute(sent, "side", [(0, 1), (1, 0)])
    own = rounded(later[0], later[1], first + side)
    new_momentum = MOMENTUM_COEF * momentum + gradient.astype(f32)
    partial = pack(jnp.concatenate([own, got], axis=0))
    pieces = partial.reshape(members, partial.shape[0] // members, BLK)
    pieces = lax.all_to_all(pieces, ("pair", "y"), split_axis=0, concat_axis=0, tiled=True)
    total = jnp.broadcast_to(jnp.sum(pieces, axis=0)[None], pieces.shape)
    packed = lax.all_to_all(total, ("pair", "y"), split_axis=0, concat_axis=0, tiled=True)
    piece = jax.ShapeDtypeStruct((rows, C), bf16)
    own, got = pl.pallas_call(
        chain_kernel,
        out_shape=(piece, piece),
        scratch_shapes=[pltpu.VMEM((C, C), f32), pltpu.VMEM((2 * rows, C), bf16)],
    )(packed.reshape(partial.shape), own, got)
    got = lax.ppermute(got, "side", [(0, 1), (1, 0)])
    both = jnp.where(side == 0, jnp.stack([own, got]), jnp.stack([got, own]))
    finished = lax.all_gather(both, "replica", axis=0, tiled=True)
    scale = 0.2 * math.sqrt(max(D, C))
    update = (scale * finished.astype(f32) + WEIGHT_DECAY * weight.astype(f32)).astype(bf16)
    return (new_momentum, update)


def solution(mesh):
    devices = mesh.devices.reshape(8, 2, 2, 8, 2)
    grid = Mesh(devices, ("y", "pair", "side", "expert", "replica"))
    placed = P("expert", ("y", "pair", "side"), None)
    return jax.shard_map(
        body,
        mesh=grid,
        in_specs=(placed, placed, placed),
        out_specs=(placed, placed),
        check_vma=False,
    )
```

```python
import math

import jax
import jax.numpy as jnp
from jax import lax
from jax.experimental import pallas as pl
from jax.experimental.pallas import tpu as pltpu
from jax.sharding import Mesh
from jax.sharding import PartitionSpec as P

D = 3584
C = 384
ITERS = 5
BLK = 128

MOMENTUM_COEF = 0.95
NORM_EPS = 1e-07
A_COEF = 3.4445
B_COEF = -4.775
C_COEF = 2.0315
WEIGHT_DECAY = 0.1

f32 = jnp.float32
bf16 = jnp.bfloat16


def dot(a, b):
    return jnp.dot(a, b, preferred_element_type=f32)


def split(value):
    high = value.astype(bf16)
    low = (value - high.astype(f32)).astype(bf16)
    return high, low


def indices():
    row = lax.broadcasted_iota(jnp.int32, (BLK, BLK), 0)
    col = lax.broadcasted_iota(jnp.int32, (BLK, BLK), 1)
    return row, col


def pack(rows):
    gram = lax.dot_general(rows, rows, (((0,), (0,)), ((), ())), preferred_element_type=f32)
    row, col = indices()

    def block(i, j):
        return lax.slice(gram, (i, j), (i + BLK, j + BLK))

    first = jnp.where(row <= col, block(0, 0), block(BLK, BLK))
    corner = (row == BLK - 1) & (col == 0)
    spare = jnp.where(corner, block(1, BLK), block(BLK, BLK + 1))
    last = jnp.where(row <= col, block(2 * BLK, 2 * BLK), spare)
    return jnp.concatenate(
        [first, block(0, BLK), block(0, 2 * BLK), block(BLK, 2 * BLK), last], axis=0
    )


def unpack(ref):
    row, col = indices()
    first, b01, b02, b12, last = [ref[i * BLK : (i + 1) * BLK] for i in range(5)]
    first_t, last_t = first.T, last.T
    b00 = jnp.where(row <= col, first, first_t)
    b22 = jnp.where(row <= col, last, last_t)
    corner = jnp.broadcast_to(last[BLK - 1 :, :1], (BLK, BLK))
    diagonal = jnp.where(row == 0, corner, pltpu.roll(last, 1, 1))
    b11 = jnp.where(row == col, diagonal, jnp.where(row > col, first, first_t))
    trace = jnp.where(row == col, b00 + b11 + b22, 0.0)
    gram = jnp.concatenate(
        [
            jnp.concatenate([b00, b01, b02], axis=1),
            jnp.concatenate([b01.T, b11, b12], axis=1),
            jnp.concatenate([b02.T, b12.T, b22], axis=1),
        ],
        axis=0,
    )
    return gram, jnp.sum(jnp.sum(trace, axis=1, keepdims=True), axis=0, keepdims=True)


def chain_kernel(packed_ref, own_ref, got_ref, own_out_ref, got_out_ref):
    count = own_ref.shape[0]
    gram, total = unpack(packed_ref)
    norm = jnp.sqrt(total) + NORM_EPS
    gram = gram / (norm * norm)
    rows = jnp.concatenate([own_ref[...], got_ref[...]], axis=0)
    iterate = (rows.astype(f32) / norm).astype(bf16)
    for iteration in range(ITERS):
        last = iteration == ITERS - 1
        high, low = split(gram)
        poly = (B_COEF * high.astype(f32) + C_COEF * dot(high, high)).astype(bf16)
        if not last:
            wide = jnp.concatenate([poly, poly], axis=1)
            half = A_COEF * gram + dot(wide, jnp.concatenate([high, low], axis=0))
        iterate = (A_COEF * iterate.astype(f32) + dot(iterate, poly)).astype(bf16)
        if not last:
            tall = jnp.concatenate([poly, poly], axis=0)
            gram = A_COEF * half + dot(jnp.concatenate(split(half), axis=1), tall)
    own_out_ref[...] = iterate[:count]
    got_out_ref[...] = iterate[count:]


def body(momentum, gradient, weight):
    rows = momentum.shape[1]
    members = 16
    side = lax.axis_index("side")
    first = 2 * lax.axis_index("replica")

    def rounded(new, old, index):
        m = lax.dynamic_index_in_dim(old, index, 0, keepdims=False)
        g = lax.dynamic_index_in_dim(new, index, 0, keepdims=False)
        return (MOMENTUM_COEF * m + g.astype(f32)).astype(bf16)

    sent = rounded(gradient, momentum, first + 1 - side)
    later = lax.optimization_barrier((gradient, momentum, sent))
    got = lax.ppermute(sent, "side", [(0, 1), (1, 0)])
    own = rounded(later[0], later[1], first + side)
    new_momentum = MOMENTUM_COEF * momentum + gradient.astype(f32)
    partial = pack(jnp.concatenate([own, got], axis=0))
    pieces = partial.reshape(members, partial.shape[0] // members, BLK)
    pieces = lax.all_to_all(pieces, ("pair", "y"), split_axis=0, concat_axis=0, tiled=True)
    total = jnp.broadcast_to(jnp.sum(pieces, axis=0)[None], pieces.shape)
    packed = lax.all_to_all(total, ("pair", "y"), split_axis=0, concat_axis=0, tiled=True)
    piece = jax.ShapeDtypeStruct((rows, C), bf16)
    own, got = pl.pallas_call(
        chain_kernel,
        out_shape=(piece, piece),
    )(packed.reshape(partial.shape), own, got)
    got = lax.ppermute(got, "side", [(0, 1), (1, 0)])
    both = jnp.where(side == 0, jnp.stack([own, got]), jnp.stack([got, own]))
    finished = lax.all_gather(both, "replica", axis=0, tiled=True)
    scale = 0.2 * math.sqrt(max(D, C))
    update = (scale * finished.astype(f32) + WEIGHT_DECAY * weight.astype(f32)).astype(bf16)
    return (new_momentum, update)


def solution(mesh):
    devices = mesh.devices.reshape(8, 2, 2, 8, 2)
    grid = Mesh(devices, ("y", "pair", "side", "expert", "replica"))
    placed = P("expert", ("y", "pair", "side"), None)
    return jax.shard_map(
        body,
        mesh=grid,
        in_specs=(placed, placed, placed),
        out_specs=(placed, placed),
        check_vma=False,
    )
```

```python
import math

import jax
import jax.numpy as jnp
from jax import lax
from jax.experimental import pallas as pl
from jax.experimental.pallas import tpu as pltpu
from jax.sharding import Mesh
from jax.sharding import PartitionSpec as P

D = 3584
C = 384
ITERS = 5
BLK = 128

MOMENTUM_COEF = 0.95
NORM_EPS = 1e-07
A_COEF = 3.4445
B_COEF = -4.775
C_COEF = 2.0315
WEIGHT_DECAY = 0.1

f32 = jnp.float32
bf16 = jnp.bfloat16


def dot(a, b):
    return jnp.dot(a, b, preferred_element_type=f32)


def split(value):
    high = value.astype(bf16)
    low = (value - high.astype(f32)).astype(bf16)
    return high, low


def indices():
    row = lax.broadcasted_iota(jnp.int32, (BLK, BLK), 0)
    col = lax.broadcasted_iota(jnp.int32, (BLK, BLK), 1)
    return row, col


def pack(rows):
    gram = lax.dot_general(rows, rows, (((0,), (0,)), ((), ())), preferred_element_type=f32)
    row, col = indices()

    def block(i, j):
        return lax.slice(gram, (i, j), (i + BLK, j + BLK))

    first = jnp.where(row <= col, block(0, 0), block(BLK, BLK))
    corner = (row == BLK - 1) & (col == 0)
    spare = jnp.where(corner, block(1, BLK), block(BLK, BLK + 1))
    last = jnp.where(row <= col, block(2 * BLK, 2 * BLK), spare)
    return jnp.concatenate(
        [first, block(0, BLK), block(0, 2 * BLK), block(BLK, 2 * BLK), last], axis=0
    )


def unpack(ref):
    row, col = indices()
    first, b01, b02, b12, last = [ref[i * BLK : (i + 1) * BLK] for i in range(5)]
    first_t, last_t = first.T, last.T
    b00 = jnp.where(row <= col, first, first_t)
    b22 = jnp.where(row <= col, last, last_t)
    corner = jnp.broadcast_to(last[BLK - 1 :, :1], (BLK, BLK))
    diagonal = jnp.where(row == 0, corner, pltpu.roll(last, 1, 1))
    b11 = jnp.where(row == col, diagonal, jnp.where(row > col, first, first_t))
    trace = jnp.where(row == col, b00 + b11 + b22, 0.0)
    gram = jnp.concatenate(
        [
            jnp.concatenate([b00, b01, b02], axis=1),
            jnp.concatenate([b01.T, b11, b12], axis=1),
            jnp.concatenate([b02.T, b12.T, b22], axis=1),
        ],
        axis=0,
    )
    return gram, jnp.sum(jnp.sum(trace, axis=1, keepdims=True), axis=0, keepdims=True)


def chain_kernel(packed_ref, own_ref, got_ref, own_out_ref, got_out_ref):
    gram, total = unpack(packed_ref)
    norm = jnp.sqrt(total) + NORM_EPS
    gram = gram / (norm * norm)
    own = (own_ref[...].astype(f32) / norm).astype(bf16)
    got = (got_ref[...].astype(f32) / norm).astype(bf16)

    def advance(rows, poly):
        return (A_COEF * rows.astype(f32) + dot(rows, poly)).astype(bf16)

    poly = None
    for iteration in range(ITERS):
        last = iteration == ITERS - 1
        high, low = split(gram)
        square = dot(high, high)
        if iteration > 0:
            own = advance(own, poly)
        poly = (B_COEF * high.astype(f32) + C_COEF * square).astype(bf16)
        if not last:
            wide = jnp.concatenate([poly, poly], axis=1)
            half = A_COEF * gram + dot(wide, jnp.concatenate([high, low], axis=0))
        got = advance(got, poly)
        if not last:
            tall = jnp.concatenate([poly, poly], axis=0)
            gram = A_COEF * half + dot(jnp.concatenate(split(half), axis=1), tall)
    own_out_ref[...] = advance(own, poly)
    got_out_ref[...] = got


def body(momentum, gradient, weight):
    rows = momentum.shape[1]
    members = 16
    side = lax.axis_index("side")
    first = 2 * lax.axis_index("replica")

    def rounded(new, old, index):
        m = lax.dynamic_index_in_dim(old, index, 0, keepdims=False)
        g = lax.dynamic_index_in_dim(new, index, 0, keepdims=False)
        return (MOMENTUM_COEF * m + g.astype(f32)).astype(bf16)

    sent = rounded(gradient, momentum, first + 1 - side)
    later = lax.optimization_barrier((gradient, momentum, sent))
    got = lax.ppermute(sent, "side", [(0, 1), (1, 0)])
    own = rounded(later[0], later[1], first + side)
    new_momentum = MOMENTUM_COEF * momentum + gradient.astype(f32)
    partial = pack(jnp.concatenate([own, got], axis=0))
    pieces = partial.reshape(members, partial.shape[0] // members, BLK)
    pieces = lax.all_to_all(pieces, ("pair", "y"), split_axis=0, concat_axis=0, tiled=True)
    total = jnp.broadcast_to(jnp.sum(pieces, axis=0)[None], pieces.shape)
    packed = lax.all_to_all(total, ("pair", "y"), split_axis=0, concat_axis=0, tiled=True)
    piece = jax.ShapeDtypeStruct((rows, C), bf16)
    own, got = pl.pallas_call(
        chain_kernel,
        out_shape=(piece, piece),
    )(packed.reshape(partial.shape), own, got)
    got = lax.ppermute(got, "side", [(0, 1), (1, 0)])
    both = jnp.where(side == 0, jnp.stack([own, got]), jnp.stack([got, own]))
    finished = lax.all_gather(both, "replica", axis=0, tiled=True)
    scale = 0.2 * math.sqrt(max(D, C))
    update = (scale * finished.astype(f32) + WEIGHT_DECAY * weight.astype(f32)).astype(bf16)
    return (new_momentum, update)


def solution(mesh):
    devices = mesh.devices.reshape(8, 2, 2, 8, 2)
    grid = Mesh(devices, ("y", "pair", "side", "expert", "replica"))
    placed = P("expert", ("y", "pair", "side"), None)
    return jax.shard_map(
        body,
        mesh=grid,
        in_specs=(placed, placed, placed),
        out_specs=(placed, placed),
        check_vma=False,
    )
```

```python
import math

import jax
import jax.numpy as jnp
from jax import lax
from jax.experimental import pallas as pl
from jax.experimental.pallas import tpu as pltpu
from jax.sharding import Mesh
from jax.sharding import PartitionSpec as P

D = 3584
C = 384
ITERS = 5
BLK = 128

MOMENTUM_COEF = 0.95
NORM_EPS = 1e-07
A_COEF = 3.4445
B_COEF = -4.775
C_COEF = 2.0315
WEIGHT_DECAY = 0.1

f32 = jnp.float32
bf16 = jnp.bfloat16


def dot(a, b):
    return jnp.dot(a, b, preferred_element_type=f32)


def split(value):
    high = value.astype(bf16)
    low = (value - high.astype(f32)).astype(bf16)
    return high, low


def indices():
    row = lax.broadcasted_iota(jnp.int32, (BLK, BLK), 0)
    col = lax.broadcasted_iota(jnp.int32, (BLK, BLK), 1)
    return row, col


def pack(rows):
    gram = lax.dot_general(rows, rows, (((0,), (0,)), ((), ())), preferred_element_type=f32)
    row, col = indices()

    def block(i, j):
        return lax.slice(gram, (i, j), (i + BLK, j + BLK))

    first = jnp.where(row <= col, block(0, 0), block(BLK, BLK))
    corner = (row == BLK - 1) & (col == 0)
    spare = jnp.where(corner, block(1, BLK), block(BLK, BLK + 1))
    last = jnp.where(row <= col, block(2 * BLK, 2 * BLK), spare)
    return jnp.concatenate(
        [first, block(0, BLK), block(0, 2 * BLK), block(BLK, 2 * BLK), last], axis=0
    )


def unpack(ref):
    row, col = indices()
    first, b01, b02, b12, last = [ref[i * BLK : (i + 1) * BLK] for i in range(5)]
    first_t, last_t = first.T, last.T
    b00 = jnp.where(row <= col, first, first_t)
    b22 = jnp.where(row <= col, last, last_t)
    corner = jnp.broadcast_to(last[BLK - 1 :, :1], (BLK, BLK))
    diagonal = jnp.where(row == 0, corner, pltpu.roll(last, 1, 1))
    b11 = jnp.where(row == col, diagonal, jnp.where(row > col, first, first_t))
    trace = jnp.where(row == col, b00 + b11 + b22, 0.0)
    gram = jnp.concatenate(
        [
            jnp.concatenate([b00, b01, b02], axis=1),
            jnp.concatenate([b01.T, b11, b12], axis=1),
            jnp.concatenate([b02.T, b12.T, b22], axis=1),
        ],
        axis=0,
    )
    return gram, jnp.sum(jnp.sum(trace, axis=1, keepdims=True), axis=0, keepdims=True)


def chain_kernel(packed_ref, own_ref, got_ref, own_out_ref, got_out_ref):
    gram, total = unpack(packed_ref)
    norm = jnp.sqrt(total) + NORM_EPS
    gram = gram * (1.0 / (norm * norm))

    def advance(rows, poly):
        return (A_COEF * rows.astype(f32) + dot(rows, poly)).astype(bf16)

    poly = None
    for iteration in range(ITERS):
        last = iteration == ITERS - 1
        high, low = split(gram)
        square = dot(high, high)
        if iteration == 0:
            own = (own_ref[...].astype(f32) / norm).astype(bf16)
            got = (got_ref[...].astype(f32) / norm).astype(bf16)
        else:
            own = advance(own, poly)
        poly = (B_COEF * high.astype(f32) + C_COEF * square).astype(bf16)
        if not last:
            wide = jnp.concatenate([poly, poly], axis=1)
            half = A_COEF * gram + dot(wide, jnp.concatenate([high, low], axis=0))
        got = advance(got, poly)
        if not last:
            tall = jnp.concatenate([poly, poly], axis=0)
            gram = A_COEF * half + dot(jnp.concatenate(split(half), axis=1), tall)
    own_out_ref[...] = advance(own, poly)
    got_out_ref[...] = got


def body(momentum, gradient, weight):
    rows = momentum.shape[1]
    members = 16
    side = lax.axis_index("side")
    first = 2 * lax.axis_index("replica")

    def rounded(new, old, index):
        m = lax.dynamic_index_in_dim(old, index, 0, keepdims=False)
        g = lax.dynamic_index_in_dim(new, index, 0, keepdims=False)
        return (MOMENTUM_COEF * m + g.astype(f32)).astype(bf16)

    sent = rounded(gradient, momentum, first + 1 - side)
    later = lax.optimization_barrier((gradient, momentum, sent))
    got = lax.ppermute(sent, "side", [(0, 1), (1, 0)])
    own = rounded(later[0], later[1], first + side)
    new_momentum = MOMENTUM_COEF * momentum + gradient.astype(f32)
    partial = pack(jnp.concatenate([own, got], axis=0))
    pieces = partial.reshape(members, partial.shape[0] // members, BLK)
    pieces = lax.all_to_all(pieces, ("pair", "y"), split_axis=0, concat_axis=0, tiled=True)
    total = jnp.broadcast_to(jnp.sum(pieces, axis=0)[None], pieces.shape)
    packed = lax.all_to_all(total, ("pair", "y"), split_axis=0, concat_axis=0, tiled=True)
    piece = jax.ShapeDtypeStruct((rows, C), bf16)
    own, got = pl.pallas_call(
        chain_kernel,
        out_shape=(piece, piece),
    )(packed.reshape(partial.shape), own, got)
    got = lax.ppermute(got, "side", [(0, 1), (1, 0)])
    both = jnp.where(side == 0, jnp.stack([own, got]), jnp.stack([got, own]))
    finished = lax.all_gather(both, "replica", axis=0, tiled=True)
    scale = 0.2 * math.sqrt(max(D, C))
    update = (scale * finished.astype(f32) + WEIGHT_DECAY * weight.astype(f32)).astype(bf16)
    return (new_momentum, update)


def solution(mesh):
    devices = mesh.devices.reshape(8, 2, 2, 8, 2)
    grid = Mesh(devices, ("y", "pair", "side", "expert", "replica"))
    placed = P("expert", ("y", "pair", "side"), None)
    return jax.shard_map(
        body,
        mesh=grid,
        in_specs=(placed, placed, placed),
        out_specs=(placed, placed),
        check_vma=False,
    )
```
